32 devices in a mesh: seq: 16 (over z, y, x), head: 2 (over core).
Axes of the slice: x: 2, y: 2, z: 4, core: 2. Of those that a mesh axis runs over, the one named last changes fastest.
Arguments:
- ssm_input: bfloat16 [8192, 3072], P('seq', 'head'), may hold values from -125 to 125
- input_map: bfloat16 [8192, 1024], P('seq', 'head'), may hold values from -0.4375 to 0.4375
- output_map: bfloat16 [8192, 1024], P('seq', 'head'), may hold values from -0.4375 to 0.4375
- decay_forward: bfloat16 [48, 8192], P('head', 'seq'), may hold values from -2 to 0
- decay_reverse: bfloat16 [48, 8192], P('head', 'seq'), may hold values from -2 to 0
- skip_gain: float32 [48], P('head'), may hold values from 0.2 to 1
- norm_gain: float32 [3072], P('head'), may hold values from 0.5 to 1.5
- scan_order: int32 [256], P('seq'), may hold values from 0 to 255, as said below
- raster_order: int32 [256], P('seq'), may hold values from 0 to 255, as said below
- grad_normed: bfloat16 [8192, 3072], P('seq', 'head'), may hold values from -6 to 6
Outputs:
- normed_output: bfloat16 [8192, 3072], P('seq', 'head')
- grad_input: bfloat16 [8192, 3072], P('seq', 'head')
The draws below stay inside these ranges and needn't reach their ends.
Inputs may be any that keep to these rules, and one draw needn't show every extreme that they name: scan_order is a permutation of the units; the units held by any index of seq, as positions 16 * e to 16 * e + 15, come one from every index of seq. raster_order is the inverse of scan_order.
All inputs are finite; a program needn't handle non-finite values.
Results may differ from the reference program's by a relative error of at most 0.011.
Values may be sent and summed in bfloat16 or wider, within the bound.
A program may use at most 128 MiB of HBM per device.

```python
import math
import jax
import jax.numpy as jnp
from jax import lax

HEAD_TOTAL = 48
HEAD_DIM = 64
STATE = 128
GROUPS = 8
SPAN = 256
TOK_DEV = 512
TOKEN_TOTAL = 8192
UNIT = 32
UNITS_DEV = 16
NUNITS = 256
FEATURES = 3072


def unit_routes(key):
    first_key, second_key = jax.random.split(key)
    senders = jax.vmap(lambda sub_key: jax.random.permutation(sub_key, UNITS_DEV))(jax.random.split(first_key, UNITS_DEV))
    picks = jax.vmap(lambda sub_key: jax.random.permutation(sub_key, UNITS_DEV))(jax.random.split(second_key, UNITS_DEV))
    dest_grid = jnp.broadcast_to(jnp.arange(UNITS_DEV)[:, None], (UNITS_DEV, UNITS_DEV))
    local_unit = picks[senders, dest_grid]
    return (senders * UNITS_DEV + local_unit).reshape(-1).astype(jnp.int32)


def draw_scan_order(key, part):
    routes = unit_routes(key)
    return routes


def draw_raster_order(key, part):
    routes = unit_routes(key)
    return jnp.argsort(routes).astype(jnp.int32)


def draw_ssm_input(key, part):
    key = jax.random.fold_in(key, 11)
    value_key, head_key, row_key = jax.random.split(key, 3)
    head_scale = jnp.exp(jax.random.uniform(head_key, (HEAD_TOTAL,), minval=math.log(0.5), maxval=math.log(5.0)))
    row_scale = jnp.exp(jax.random.uniform(row_key, (TOKEN_TOTAL,), minval=math.log(0.5), maxval=math.log(5.0)))
    raw_values = jnp.clip(jax.random.normal(value_key, (TOKEN_TOTAL, FEATURES)), -5.0, 5.0)
    column_scale = jnp.repeat(head_scale, HEAD_DIM)
    return (raw_values * column_scale[None, :] * row_scale[:, None]).astype(jnp.bfloat16)


def decay_law(key, fast_share):
    random_key_list = jax.random.split(key, 8)
    block_count = TOKEN_TOTAL // TOK_DEV
    fast_heads = jax.random.randint(random_key_list[0], (HEAD_TOTAL,), 0, 8) < fast_share
    fast_blocks = jax.random.randint(random_key_list[7], (HEAD_TOTAL, block_count), 0, 2) == 0
    fast_mask = jnp.logical_and(fast_heads[:, None], fast_blocks)
    fast_rate = jax.random.uniform(random_key_list[1], (HEAD_TOTAL,), minval=1.0 / 50.0, maxval=1.0 / 30.0)
    slow_rate = jax.random.uniform(random_key_list[2], (HEAD_TOTAL,), minval=0.2, maxval=0.6) * math.log(2.0) / TOKEN_TOTAL
    block_rate = jnp.where(fast_mask, fast_rate[:, None], slow_rate[:, None])
    roughness = jnp.exp(jax.random.uniform(random_key_list[3], (HEAD_TOTAL, TOKEN_TOTAL), minval=-math.log(2.0), maxval=math.log(2.0)))
    block_factor = jnp.exp(jax.random.uniform(random_key_list[4], (block_count,), minval=-math.log(2.0), maxval=math.log(2.0)))
    constant_level = -jnp.repeat(block_rate * block_factor[None, :], TOK_DEV, axis=1) * roughness
    spike_position = jax.random.randint(random_key_list[5], (HEAD_TOTAL, 2), 0, TOKEN_TOTAL)
    spike_length = jnp.log(jax.random.uniform(random_key_list[6], (HEAD_TOTAL, 2), minval=0.5, maxval=0.8))
    head_numbers = jnp.broadcast_to(jnp.arange(HEAD_TOTAL)[:, None], (HEAD_TOTAL, 2))
    spike_list = jnp.zeros((HEAD_TOTAL, TOKEN_TOTAL), jnp.float32).at[head_numbers, spike_position].add(spike_length)
    return (constant_level + spike_list).astype(jnp.bfloat16)


def draw_decay_forward(key, part):
    key = jax.random.fold_in(key, 21)
    return decay_law(key, 4)


def draw_decay_reverse(key, part):
    key = jax.random.fold_in(key, 22)
    return decay_law(key, 4)


def block_levels(rng, dims, shards, least, high):
    gain, own = 1.0, jax.random.fold_in(rng, 6)
    for dim, parts in shards:
        draws = jnp.exp(jax.random.uniform(jax.random.fold_in(own, dim), (parts,), jnp.float32, least / len(shards), high / len(shards)))
        gain = gain * jnp.repeat(draws, dims[dim] // parts).reshape([-1 if axis == dim else 1 for axis in range(len(dims))])
    return gain


def scatter_about(own_key, dims, scale, most, cuts=(), held_as=jnp.bfloat16):
    level = block_levels(own_key, dims, cuts, -0.22, 0.18) if cuts else 1.0
    drawn = jax.random.normal(own_key, dims, jnp.float32) * scale * level
    return jnp.minimum(jnp.maximum(drawn, -most), most).astype(held_as)


def setup_inputs(seed: int = 0) -> dict:
    seeds = jax.random.split(jax.random.key(seed), 11)
    return {
        "ssm_input": draw_ssm_input(jax.random.fold_in(seeds[10], 71), 0),
        "input_map": scatter_about(seeds[1], (TOKEN_TOTAL, GROUPS * STATE), 0.03, 0.4375, ((0, 16), (1, 2))),
        "output_map": scatter_about(seeds[2], (TOKEN_TOTAL, GROUPS * STATE), 0.03, 0.4375, ((0, 16), (1, 2))),
        "decay_forward": draw_decay_forward(jax.random.fold_in(seeds[10], 71), 0),
        "decay_reverse": draw_decay_reverse(jax.random.fold_in(seeds[10], 71), 0),
        "skip_gain": jnp.clip(0.2 + 0.8 * jax.random.uniform(seeds[5], (HEAD_TOTAL,), jnp.float32) ** block_levels(seeds[5], (HEAD_TOTAL,), ((0, 2),), -0.2, 0.2), 0.2, 1.0),
        "norm_gain": jnp.clip(1.0 + 0.1 * jax.random.normal(seeds[6], (FEATURES,), jnp.float32), 0.5, 1.5),
        "scan_order": draw_scan_order(jax.random.fold_in(seeds[10], 71), 0),
        "raster_order": draw_raster_order(jax.random.fold_in(seeds[10], 71), 0),
        "grad_normed": scatter_about(seeds[9], (TOKEN_TOTAL, FEATURES), 1.0, 6.0, ((0, 16), (1, 2))),
    }


EPSILON = 1e-05
HIGHEST = lax.Precision.HIGHEST

def span_update(state_in, pieces, reverse):
    value_span, key_span, query_span, decay_span = pieces
    per_group = HEAD_TOTAL // GROUPS
    cumulative = jnp.cumsum(decay_span.astype(jnp.float32), axis=1)
    key_rows = key_span.astype(jnp.float32)
    query_rows = query_span.astype(jnp.float32)
    values = value_span.astype(jnp.float32)
    scores = jnp.einsum('ign,jgn->gij', query_rows, key_rows, precision=HIGHEST)
    scores = jnp.repeat(scores, per_group, axis=0)
    spread = cumulative[:, :, None] - cumulative[:, None, :]
    row_ids = lax.broadcasted_iota(jnp.int32, (SPAN, SPAN), 0)
    col_ids = lax.broadcasted_iota(jnp.int32, (SPAN, SPAN), 1)
    span_end = cumulative[:, -1]
    if reverse:
        allowed = col_ids >= row_ids
        damping = jnp.exp(jnp.minimum(-spread, 0.0))
        key_weight = jnp.exp(cumulative)
        query_weight = jnp.exp(span_end[:, None] - cumulative)
    else:
        allowed = col_ids <= row_ids
        damping = jnp.exp(jnp.minimum(spread, 0.0))
        key_weight = jnp.exp(span_end[:, None] - cumulative)
        query_weight = jnp.exp(cumulative)
    weights = jnp.where(allowed[None], scores * damping, 0.0)
    weights = lax.optimization_barrier(weights.astype(jnp.bfloat16)).astype(jnp.float32)
    inner_part = jnp.einsum('hij,jhp->ihp', weights, values, precision=HIGHEST)
    head_queries = jnp.repeat(query_rows, per_group, axis=1)
    head_keys = jnp.repeat(key_rows, per_group, axis=1)
    state_bf = lax.optimization_barrier(state_in.astype(jnp.bfloat16)).astype(jnp.float32)
    outer_part = jnp.einsum('ihn,hnp->ihp', head_queries, state_bf, precision=HIGHEST)
    outer_part = outer_part * query_weight.T[:, :, None]
    scaled_keys = head_keys * key_weight.T[:, :, None]
    scaled_keys = lax.optimization_barrier(scaled_keys.astype(jnp.bfloat16)).astype(jnp.float32)
    contrib = jnp.einsum('jhn,jhp->hnp', scaled_keys, values, precision=HIGHEST)
    state_out = jnp.exp(span_end)[:, None, None] * state_in + contrib
    return (state_out, inner_part + outer_part)

def scan_all(values, key_rows, query_rows, log_decay, reverse):
    length = values.shape[0]
    span_count = length // SPAN
    value_spans = values.reshape(span_count, SPAN, HEAD_TOTAL, HEAD_DIM)
    key_spans = key_rows.reshape(span_count, SPAN, GROUPS, STATE)
    query_spans = query_rows.reshape(span_count, SPAN, GROUPS, STATE)
    decay_spans = log_decay.reshape(HEAD_TOTAL, span_count, SPAN).transpose(1, 0, 2)
    start_state = jnp.zeros((HEAD_TOTAL, STATE, HEAD_DIM), jnp.float32)

    def advance(state_in, pieces):
        return span_update(state_in, pieces, reverse)
    _, outputs = lax.scan(advance, start_state, (value_spans, key_spans, query_spans, decay_spans), reverse=reverse)
    return outputs.reshape(length, HEAD_TOTAL * HEAD_DIM)

def to_scan(array, scan_order):
    return array.reshape(NUNITS, UNIT, -1)[scan_order].reshape(array.shape)

def to_raster(array, raster_order):
    return array.reshape(NUNITS, UNIT, -1)[raster_order].reshape(array.shape)

def reference(ssm_input, input_map, output_map, decay_forward, decay_reverse, skip_gain, norm_gain, scan_order, raster_order, grad_normed):
    scan_input = to_scan(ssm_input, scan_order)
    scan_in_map = to_scan(input_map, scan_order)
    scan_out_map = to_scan(output_map, scan_order)
    y_forward = scan_all(ssm_input, input_map, output_map, decay_forward, False).astype(jnp.bfloat16)
    y_reverse_scan = scan_all(scan_input, scan_in_map, scan_out_map, decay_reverse, True).astype(jnp.bfloat16)
    y_reverse = to_raster(y_reverse_scan, raster_order)
    skip_cols = jnp.repeat(skip_gain, HEAD_DIM)
    combined = y_forward.astype(jnp.float32) + y_reverse.astype(jnp.float32) + skip_cols * ssm_input.astype(jnp.float32)
    inv_rms = lax.rsqrt(lax.optimization_barrier(jnp.sum(combined * combined, axis=1)) / FEATURES + EPSILON)
    normed_output = (combined * inv_rms[:, None] * norm_gain).astype(jnp.bfloat16)
    scaled_grad = norm_gain * grad_normed.astype(jnp.float32)
    inner_sum = lax.optimization_barrier(jnp.sum(combined * scaled_grad, axis=1))
    grad_combined = inv_rms[:, None] * scaled_grad - combined * (inv_rms ** 3 * inner_sum / FEATURES)[:, None]
    grad_combined = grad_combined.astype(jnp.bfloat16)
    grad_forward = scan_all(grad_combined, output_map, input_map, decay_forward, True).astype(jnp.bfloat16)
    grad_reverse_scan = scan_all(to_scan(grad_combined, scan_order), scan_out_map, scan_in_map, decay_reverse, False).astype(jnp.bfloat16)
    grad_reverse = to_raster(grad_reverse_scan, raster_order)
    grad_input = grad_forward.astype(jnp.float32) + grad_reverse.astype(jnp.float32) + skip_cols * grad_combined.astype(jnp.float32)
    return (normed_output, grad_input.astype(jnp.bfloat16))
```

```python
import functools

import jax
import jax.numpy as jnp
from jax import lax
from jax.experimental import pallas as pl
from jax.experimental.pallas import tpu as pltpu
from jax.sharding import PartitionSpec as P

HEAD_DIM = 64
STATE = 128
SPAN = 256
FEATURES = 3072
PAD = 8
LANES = 128
EPSILON = 1e-05
F32 = jnp.float32
BF16 = jnp.bfloat16


def triangle(lower):
    rows = lax.broadcasted_iota(jnp.int32, (SPAN, SPAN), 0)
    cols = lax.broadcasted_iota(jnp.int32, (SPAN, SPAN), 1)
    return cols <= rows if lower else cols >= rows


def spread_pair(columns, pair):
    shape = (columns.shape[0], LANES)
    lane = lax.broadcasted_iota(jnp.int32, shape, 1)
    return jnp.where(
        lane < HEAD_DIM, columns[:, 2 * pair : 2 * pair + 1], columns[:, 2 * pair + 1 : 2 * pair + 2]
    )


def spread_heads(columns, pairs):
    return jnp.concatenate([spread_pair(columns, pair) for pair in range(pairs)], axis=1)


def running_columns(decay):
    ones = jnp.where(triangle(True), 1.0, 0.0).astype(BF16)
    return lax.dot_general(ones, decay, (((1,), (1,)), ((), ())), preferred_element_type=F32)


def running_rows(decay):
    ones = jnp.where(triangle(False), 1.0, 0.0).astype(BF16)
    return jnp.dot(decay, ones, preferred_element_type=F32)


def states_kernel(reverse, spans, v_ref, k_ref, decay_ref, before_ref, total_ref):
    pairs = v_ref.shape[1] // LANES
    order = range(spans)
    run = None
    for span in order[::-1] if reverse else order:
        rows = slice(span * SPAN, (span + 1) * SPAN)
        cum = running_columns(decay_ref[0, :, rows].astype(BF16))
        end = cum[SPAN - 1 : SPAN]
        weight = jnp.exp(cum) if reverse else jnp.exp(end - cum)
        scaled = (v_ref[rows, :].astype(F32) * spread_heads(weight, pairs)).astype(BF16)
        state = lax.dot_general(
            k_ref[rows, :], scaled, (((0,), (0,)), ((), ())), preferred_element_type=F32
        )
        if run is None:
            before_ref[span] = jnp.zeros_like(state)
            run = state
        else:
            before_ref[span] = run
            run = run * spread_heads(jnp.exp(end), pairs) + state
    total_ref[...] = run.astype(BF16)


def inner_kernel(reverse, spans, v_ref, k_ref, q_ref, decay_ref, out_ref):
    pairs = v_ref.shape[1] // LANES
    allowed = triangle(not reverse)
    lane = lax.broadcasted_iota(jnp.int32, (SPAN, LANES), 1)
    for span in range(spans):
        rows = slice(span * SPAN, (span + 1) * SPAN)
        decay = decay_ref[0, :, rows].astype(BF16)
        cum_col = running_columns(decay)
        cum_row = running_rows(decay)
        scores = lax.dot_general(
            q_ref[rows, :], k_ref[rows, :], (((1,), (1,)), ((), ())), preferred_element_type=F32
        )
        scores = jnp.where(allowed, scores, 0.0)
        for pair in range(pairs):
            values = v_ref[rows, pair * LANES : (pair + 1) * LANES]
            parts = []
            for head in (2 * pair, 2 * pair + 1):
                col, row = cum_col[:, head : head + 1], cum_row[head : head + 1, :]
                gap = row - col if reverse else col - row
                weights = (scores * jnp.exp(jnp.minimum(gap, 0.0))).astype(BF16)
                parts.append(jnp.dot(weights, values, preferred_element_type=F32))
            out_ref[rows, pair * LANES : (pair + 1) * LANES] = jnp.where(
                lane < HEAD_DIM, parts[0], parts[1]
            )


def finish_kernel(reverse, spans, inner_ref, q_ref, decay_ref, before_ref, incoming_ref, out_ref):
    pairs = inner_ref.shape[1] // LANES
    order = range(spans)
    incoming = incoming_ref[...].astype(F32)
    passed = None
    for span in order[::-1] if reverse else order:
        rows = slice(span * SPAN, (span + 1) * SPAN)
        cum = running_columns(decay_ref[0, :, rows].astype(BF16))
        end = cum[SPAN - 1 : SPAN]
        weight = jnp.exp(end - cum) if reverse else jnp.exp(cum)
        if passed is None:
            entering = incoming
            passed = end
        else:
            entering = before_ref[span] + incoming * spread_heads(jnp.exp(passed), pairs)
            passed = passed + end
        outer = jnp.dot(q_ref[rows, :], entering.astype(BF16), preferred_element_type=F32)
        out_ref[rows, :] = (inner_ref[rows, :] + outer * spread_heads(weight, pairs)).astype(BF16)


class Scan:
    def __init__(self, values, keys, queries, decay, width, reverse):
        self.decay, self.reverse, self.width = decay, reverse, width
        self.groups = decay.shape[0]
        self.tokens = decay.shape[2]
        self.spans = self.tokens // SPAN
        self.cols = width // self.groups
        self.values, self.keys, self.queries = values, keys, queries

    def cut(self, operand, size):
        array, first = operand
        base = first // size
        return array, pl.BlockSpec((self.tokens, size), lambda g: (0, base + g))

    def call(self, body, operands, outs, out_specs, flops):
        arrays, specs = zip(*operands)
        shapes = jax.tree.leaves(outs)
        moved = sum(s.size * s.dtype.itemsize for s in shapes) * 2
        return pl.pallas_call(
            functools.partial(body, self.reverse, self.spans),
            grid=(self.groups,),
            in_specs=list(specs),
            out_specs=out_specs,
            out_shape=outs,
            compiler_params=pltpu.CompilerParams(vmem_limit_bytes=48 * 2**20),
            cost_estimate=pl.CostEstimate(flops=flops, bytes_accessed=moved, transcendentals=0),
        )(*arrays)

    def decay_cut(self):
        return self.decay, pl.BlockSpec((1, PAD, self.tokens), lambda g: (g, 0, 0))

    def states(self):
        wide = pl.BlockSpec((STATE, self.cols), lambda g: (0, g))
        deep = pl.BlockSpec((self.spans, STATE, self.cols), lambda g: (0, 0, g))
        self.before, total = self.call(
            states_kernel,
            [self.cut(self.values, self.cols), self.cut(self.keys, STATE), self.decay_cut()],
            (
                jax.ShapeDtypeStruct((self.spans, STATE, self.width), F32),
                jax.ShapeDtypeStruct((STATE, self.width), BF16),
            ),
            (deep, wide),
            2 * self.tokens * STATE * self.width,
        )
        return total

    def inner(self):
        self.near = self.call(
            inner_kernel,
            [
                self.cut(self.values, self.cols),
                self.cut(self.keys, STATE),
                self.cut(self.queries, STATE),
                self.decay_cut(),
            ],
            jax.ShapeDtypeStruct((self.tokens, self.width), F32),
            pl.BlockSpec((self.tokens, self.cols), lambda g: (0, g)),
            8 * self.tokens * SPAN * self.width,
        )

    def finish(self, incoming):
        wide = pl.BlockSpec((STATE, self.cols), lambda g: (0, g))
        deep = pl.BlockSpec((self.spans, STATE, self.cols), lambda g: (0, 0, g))
        rows = pl.BlockSpec((self.tokens, self.cols), lambda g: (0, g))
        return self.call(
            finish_kernel,
            [
                (self.near, rows),
                self.cut(self.queries, STATE),
                self.decay_cut(),
                (self.before, deep),
                (incoming, wide),
            ],
            jax.ShapeDtypeStruct((self.tokens, self.width), BF16),
            rows,
            2 * self.tokens * STATE * self.width,
        )


def prefix_kernel(reverse, arrived_ref, factor_ref, out_ref):
    count = arrived_ref.shape[0]
    run = jnp.zeros(arrived_ref.shape[1:], F32)
    order = range(count)
    for index in order[::-1] if reverse else order:
        out_ref[index] = run.astype(BF16)
        run = run * factor_ref[index] + arrived_ref[index].astype(F32)


def carried(total, factors, reverse):
    count = lax.axis_size("seq")
    pieces = total.reshape(count, STATE // count, -1)
    arrived = lax.all_to_all(pieces, "seq", split_axis=0, concat_axis=0, tiled=True)
    composed = pl.pallas_call(
        functools.partial(prefix_kernel, reverse),
        out_shape=jax.ShapeDtypeStruct(arrived.shape, BF16),
    )(arrived, factors)
    back = lax.all_to_all(composed, "seq", split_axis=0, concat_axis=0, tiled=True)
    return back.reshape(total.shape)


def gather_kernel(counts, index_ref, *refs):
    sources, out_ref, sems = refs[: len(counts)], refs[-2], refs[-1]
    copies = []
    for unit in range(out_ref.shape[0]):
        first = 0
        for place, (source, width) in enumerate(zip(sources, counts)):
            copy = pltpu.make_async_copy(
                source.at[index_ref[unit]],
                out_ref.at[unit, :, pl.ds(first, width)],
                sems.at[unit, place],
            )
            copy.start()
            copies.append(copy)
            first += width
    for copy in copies:
        copy.wait()


def gathered(arrays, index):
    widths = tuple(array.shape[2] for array in arrays)
    units, rows = arrays[0].shape[:2]
    hbm = pl.BlockSpec(memory_space=pl.ANY)
    return pl.pallas_call(
        functools.partial(gather_kernel, widths),
        in_specs=[pl.BlockSpec(memory_space=pltpu.SMEM)] + [hbm] * len(arrays),
        out_specs=hbm,
        out_shape=jax.ShapeDtypeStruct((units, rows, sum(widths)), arrays[0].dtype),
        scratch_shapes=[pltpu.SemaphoreType.DMA((units, len(arrays)))],
    )(index, *arrays)


def inverse(order):
    count = order.shape[0]
    spots = jnp.arange(count, dtype=jnp.int32)
    return jnp.sum(jnp.where(order[None, :] == spots[:, None], spots[None, :], 0), axis=1)


def shards(
    ssm_input,
    input_map,
    output_map,
    decay_forward,
    decay_reverse,
    skip_gain,
    norm_gain,
    scan_order,
    raster_order,
    grad_normed,
):
    unit_count = scan_order.shape[0]
    tok_rows, width = ssm_input.shape
    unit_rows = tok_rows // unit_count
    maps = input_map.shape[1]
    groups = maps // STATE
    heads = decay_forward.shape[0]
    raster_dest = raster_order // unit_count
    scan_source = scan_order // unit_count
    send_scan = inverse(raster_dest)
    send_raster = inverse(scan_source)

    def units(array):
        return array.reshape(unit_count, unit_rows, -1)

    def moved(arrays, send_index, recv_index):
        outgoing = gathered([units(array) for array in arrays], send_index)
        arrived = lax.all_to_all(outgoing, "seq", split_axis=0, concat_axis=0, tiled=True)
        return gathered([arrived], recv_index).reshape(tok_rows, -1)

    def to_scan(*arrays):
        return moved(arrays, send_scan, scan_source)

    def to_raster(array):
        return moved([array], send_raster, raster_dest)

    def padded(decay):
        wide = decay.astype(F32).reshape(groups, heads // groups, tok_rows)
        return jnp.pad(wide, ((0, 0), (0, PAD - heads // groups), (0, 0)))

    sums = jnp.stack([decay_forward, decay_reverse]).astype(F32).sum(axis=2)
    all_sums = lax.all_gather(sums, "seq", axis=0)
    factors = jnp.repeat(jnp.exp(all_sums), HEAD_DIM, axis=2)
    forward_factors, reverse_factors = factors[:, 0:1], factors[:, 1:2]
    decay_f, decay_r = padded(decay_forward), padded(decay_reverse)

    joined = to_scan(ssm_input, input_map, output_map)
    keys_at, queries_at = width, width + maps

    ahead = Scan((ssm_input, 0), (input_map, 0), (output_map, 0), decay_f, width, False)
    ahead_in = carried(ahead.states(), forward_factors, False)
    ahead.inner()
    y_forward = ahead.finish(ahead_in)

    behind = Scan((joined, 0), (joined, keys_at), (joined, queries_at), decay_r, width, True)
    behind_in = carried(behind.states(), reverse_factors, True)
    behind.inner()
    y_reverse = to_raster(behind.finish(behind_in))

    skip_cols = jnp.repeat(skip_gain, HEAD_DIM)
    combined = (
        y_forward.astype(F32) + y_reverse.astype(F32) + skip_cols * ssm_input.astype(F32)
    )
    scaled_grad = norm_gain * grad_normed.astype(F32)
    both = jnp.stack(
        [jnp.sum(combined * combined, axis=1), jnp.sum(combined * scaled_grad, axis=1)]
    )
    squares, inner_sum = lax.psum(both, "head")
    inv_rms = lax.rsqrt(squares / FEATURES + EPSILON)
    normed_output = (combined * inv_rms[:, None] * norm_gain).astype(BF16)
    grad_combined = (
        inv_rms[:, None] * scaled_grad - combined * (inv_rms**3 * inner_sum / FEATURES)[:, None]
    ).astype(BF16)

    grad_scan = to_scan(grad_combined)
    ahead_grad = Scan((grad_combined, 0), (output_map, 0), (input_map, 0), decay_f, width, True)
    ahead_grad_in = carried(ahead_grad.states(), forward_factors, True)
    ahead_grad.inner()
    grad_forward = ahead_grad.finish(ahead_grad_in)

    behind_grad = Scan((grad_scan, 0), (joined, queries_at), (joined, keys_at), decay_r, width, False)
    behind_grad_in = carried(behind_grad.states(), reverse_factors, False)
    behind_grad.inner()
    grad_reverse = to_raster(behind_grad.finish(behind_grad_in))

    grad_input = (
        grad_forward.astype(F32)
        + grad_reverse.astype(F32)
        + skip_cols * grad_combined.astype(F32)
    )
    return (normed_output, grad_input.astype(BF16))


def solution(mesh):
    return jax.shard_map(
        shards,
        mesh=mesh,
        in_specs=(
            P("seq", "head"),
            P("seq", "head"),
            P("seq", "head"),
            P("head", "seq"),
            P("head", "seq"),
            P("head"),
            P("head"),
            P("seq"),
            P("seq"),
            P("seq", "head"),
        ),
        out_specs=(P("seq", "head"), P("seq", "head")),
        check_vma=False,
    )
```

```python
import functools

import jax
import jax.numpy as jnp
from jax import lax
from jax.experimental import pallas as pl
from jax.experimental.pallas import tpu as pltpu
from jax.sharding import PartitionSpec as P

HEAD_DIM = 64
STATE = 128
SPAN = 256
FEATURES = 3072
PAD = 8
LANES = 128
EPSILON = 1e-05
F32 = jnp.float32
BF16 = jnp.bfloat16


def triangle(lower):
    rows = lax.broadcasted_iota(jnp.int32, (SPAN, SPAN), 0)
    cols = lax.broadcasted_iota(jnp.int32, (SPAN, SPAN), 1)
    return cols <= rows if lower else cols >= rows


def spread_pair(columns, pair):
    shape = (columns.shape[0], LANES)
    lane = lax.broadcasted_iota(jnp.int32, shape, 1)
    return jnp.where(
        lane < HEAD_DIM, columns[:, 2 * pair : 2 * pair + 1], columns[:, 2 * pair + 1 : 2 * pair + 2]
    )


def spread_heads(columns, pairs):
    return jnp.concatenate([spread_pair(columns, pair) for pair in range(pairs)], axis=1)


def running_columns(decay):
    ones = jnp.where(triangle(True), 1.0, 0.0).astype(BF16)
    return lax.dot_general(ones, decay, (((1,), (1,)), ((), ())), preferred_element_type=F32)


def running_rows(decay):
    ones = jnp.where(triangle(False), 1.0, 0.0).astype(BF16)
    return jnp.dot(decay, ones, preferred_element_type=F32)


def states_kernel(reverse, spans, v_ref, k_ref, decay_ref, before_ref, total_ref):
    pairs = v_ref.shape[1] // LANES
    order = range(spans)
    run = None
    for span in order[::-1] if reverse else order:
        rows = slice(span * SPAN, (span + 1) * SPAN)
        cum = running_columns(decay_ref[0, :, rows].astype(BF16))
        end = cum[SPAN - 1 : SPAN]
        weight = jnp.exp(cum) if reverse else jnp.exp(end - cum)
        scaled = (v_ref[rows, :].astype(F32) * spread_heads(weight, pairs)).astype(BF16)
        state = lax.dot_general(
            k_ref[rows, :], scaled, (((0,), (0,)), ((), ())), preferred_element_type=F32
        )
        if run is None:
            before_ref[span] = jnp.zeros_like(state)
            run = state
        else:
            before_ref[span] = run
            run = run * spread_heads(jnp.exp(end), pairs) + state
    total_ref[...] = run.astype(BF16)


def inner_kernel(reverse, spans, v_ref, k_ref, q_ref, decay_ref, out_ref):
    pairs = v_ref.shape[1] // LANES
    allowed = triangle(not reverse)
    lane = lax.broadcasted_iota(jnp.int32, (SPAN, LANES), 1)
    for span in range(spans):
        rows = slice(span * SPAN, (span + 1) * SPAN)
        decay = decay_ref[0, :, rows].astype(BF16)
        cum_col = running_columns(decay)
        cum_row = running_rows(decay)
        scores = lax.dot_general(
            q_ref[rows, :], k_ref[rows, :], (((1,), (1,)), ((), ())), preferred_element_type=F32
        )
        scores = jnp.where(allowed, scores, 0.0)
        for pair in range(pairs):
            values = v_ref[rows, pair * LANES : (pair + 1) * LANES]
            parts = []
            for head in (2 * pair, 2 * pair + 1):
                col, row = cum_col[:, head : head + 1], cum_row[head : head + 1, :]
                gap = row - col if reverse else col - row
                weights = (scores * jnp.exp(jnp.minimum(gap, 0.0))).astype(BF16)
                parts.append(jnp.dot(weights, values, preferred_element_type=F32))
            out_ref[rows, pair * LANES : (pair + 1) * LANES] = jnp.where(
                lane < HEAD_DIM, parts[0], parts[1]
            )


def finish_kernel(reverse, spans, inner_ref, q_ref, decay_ref, before_ref, incoming_ref, out_ref):
    pairs = inner_ref.shape[1] // LANES
    order = range(spans)
    incoming = incoming_ref[...].astype(F32)
    passed = None
    for span in order[::-1] if reverse else order:
        rows = slice(span * SPAN, (span + 1) * SPAN)
        cum = running_columns(decay_ref[0, :, rows].astype(BF16))
        end = cum[SPAN - 1 : SPAN]
        weight = jnp.exp(end - cum) if reverse else jnp.exp(cum)
        if passed is None:
            entering = incoming
            passed = end
        else:
            entering = before_ref[span] + incoming * spread_heads(jnp.exp(passed), pairs)
            passed = passed + end
        outer = jnp.dot(q_ref[rows, :], entering.astype(BF16), preferred_element_type=F32)
        out_ref[rows, :] = (inner_ref[rows, :] + outer * spread_heads(weight, pairs)).astype(BF16)


class Scan:
    def __init__(self, values, keys, queries, decay, width, reverse):
        self.decay, self.reverse, self.width = decay, reverse, width
        self.groups = decay.shape[0]
        self.tokens = decay.shape[2]
        self.spans = self.tokens // SPAN
        self.cols = width // self.groups
        self.values, self.keys, self.queries = values, keys, queries

    def cut(self, operand, size):
        array, first = operand
        base = first // size
        return array, pl.BlockSpec((self.tokens, size), lambda g: (0, base + g))

    def call(self, body, operands, outs, out_specs, flops):
        arrays, specs = zip(*operands)
        shapes = jax.tree.leaves(outs)
        moved = sum(s.size * s.dtype.itemsize for s in shapes) * 2
        return pl.pallas_call(
            functools.partial(body, self.reverse, self.spans),
            grid=(self.groups,),
            in_specs=list(specs),
            out_specs=out_specs,
            out_shape=outs,
            compiler_params=pltpu.CompilerParams(vmem_limit_bytes=48 * 2**20),
            cost_estimate=pl.CostEstimate(flops=flops, bytes_accessed=moved, transcendentals=0),
        )(*arrays)

    def decay_cut(self):
        return self.decay, pl.BlockSpec((1, PAD, self.tokens), lambda g: (g, 0, 0))

    def states(self):
        wide = pl.BlockSpec((STATE, self.cols), lambda g: (0, g))
        deep = pl.BlockSpec((self.spans, STATE, self.cols), lambda g: (0, 0, g))
        self.before, total = self.call(
            states_kernel,
            [self.cut(self.values, self.cols), self.cut(self.keys, STATE), self.decay_cut()],
            (
                jax.ShapeDtypeStruct((self.spans, STATE, self.width), F32),
                jax.ShapeDtypeStruct((STATE, self.width), BF16),
            ),
            (deep, wide),
            2 * self.tokens * STATE * self.width,
        )
        return total

    def inner(self):
        self.near = self.call(
            inner_kernel,
            [
                self.cut(self.values, self.cols),
                self.cut(self.keys, STATE),
                self.cut(self.queries, STATE),
                self.decay_cut(),
            ],
            jax.ShapeDtypeStruct((self.tokens, self.width), F32),
            pl.BlockSpec((self.tokens, self.cols), lambda g: (0, g)),
            8 * self.tokens * SPAN * self.width,
        )

    def finish(self, incoming):
        wide = pl.BlockSpec((STATE, self.cols), lambda g: (0, g))
        deep = pl.BlockSpec((self.spans, STATE, self.cols), lambda g: (0, 0, g))
        rows = pl.BlockSpec((self.tokens, self.cols), lambda g: (0, g))
        return self.call(
            finish_kernel,
            [
                (self.near, rows),
                self.cut(self.queries, STATE),
                self.decay_cut(),
                (self.before, deep),
                (incoming, wide),
            ],
            jax.ShapeDtypeStruct((self.tokens, self.width), BF16),
            rows,
            2 * self.tokens * STATE * self.width,
        )


def prefix_kernel(reverse, arrived_ref, factor_ref, out_ref):
    count = arrived_ref.shape[0]
    run = jnp.zeros(arrived_ref.shape[1:], F32)
    order = range(count)
    for index in order[::-1] if reverse else order:
        out_ref[index] = run.astype(BF16)
        run = run * factor_ref[index] + arrived_ref[index].astype(F32)


def carried(total, factors, reverse):
    count = lax.axis_size("seq")
    pieces = total.reshape(count, STATE // count, -1)
    arrived = lax.all_to_all(pieces, "seq", split_axis=0, concat_axis=0, tiled=True)
    composed = pl.pallas_call(
        functools.partial(prefix_kernel, reverse),
        out_shape=jax.ShapeDtypeStruct(arrived.shape, BF16),
    )(arrived, factors)
    back = lax.all_to_all(composed, "seq", split_axis=0, concat_axis=0, tiled=True)
    return back.reshape(total.shape)


def gather_kernel(counts, index_ref, *refs):
    sources, out_ref = refs[: len(counts)], refs[-1]

    @pl.loop(0, out_ref.shape[0])
    def _(unit):
        first = 0
        for source, width in zip(sources, counts):
            out_ref[unit, :, first : first + width] = source[index_ref[unit]]
            first += width


def gathered(arrays, index):
    widths = tuple(array.shape[2] for array in arrays)
    units, rows = arrays[0].shape[:2]
    whole = pl.BlockSpec(memory_space=pltpu.VMEM)
    return pl.pallas_call(
        functools.partial(gather_kernel, widths),
        in_specs=[pl.BlockSpec(memory_space=pltpu.SMEM)] + [whole] * len(arrays),
        out_specs=whole,
        out_shape=jax.ShapeDtypeStruct((units, rows, sum(widths)), arrays[0].dtype),
        compiler_params=pltpu.CompilerParams(vmem_limit_bytes=48 * 2**20),
    )(index, *arrays)


def inverse(order):
    count = order.shape[0]
    spots = jnp.arange(count, dtype=jnp.int32)
    return jnp.sum(jnp.where(order[None, :] == spots[:, None], spots[None, :], 0), axis=1)


def shards(
    ssm_input,
    input_map,
    output_map,
    decay_forward,
    decay_reverse,
    skip_gain,
    norm_gain,
    scan_order,
    raster_order,
    grad_normed,
):
    unit_count = scan_order.shape[0]
    tok_rows, width = ssm_input.shape
    unit_rows = tok_rows // unit_count
    maps = input_map.shape[1]
    groups = maps // STATE
    heads = decay_forward.shape[0]
    raster_dest = raster_order // unit_count
    scan_source = scan_order // unit_count
    send_scan = inverse(raster_dest)
    send_raster = inverse(scan_source)

    def units(array):
        return array.reshape(unit_count, unit_rows, -1)

    def moved(arrays, send_index, recv_index):
        outgoing = gathered([units(array) for array in arrays], send_index)
        arrived = lax.all_to_all(outgoing, "seq", split_axis=0, concat_axis=0, tiled=True)
        return gathered([arrived], recv_index).reshape(tok_rows, -1)

    def to_scan(*arrays):
        return moved(arrays, send_scan, scan_source)

    def to_raster(array):
        return moved([array], send_raster, raster_dest)

    def padded(decay):
        wide = decay.astype(F32).reshape(groups, heads // groups, tok_rows)
        return jnp.pad(wide, ((0, 0), (0, PAD - heads // groups), (0, 0)))

    sums = jnp.stack([decay_forward, decay_reverse]).astype(F32).sum(axis=2)
    copies = jnp.broadcast_to(sums[None], (lax.axis_size("seq"), *sums.shape))
    all_sums = lax.all_to_all(copies, "seq", split_axis=0, concat_axis=0, tiled=True)
    factors = jnp.repeat(jnp.exp(all_sums), HEAD_DIM, axis=2)
    forward_factors, reverse_factors = factors[:, 0:1], factors[:, 1:2]
    decay_f, decay_r = padded(decay_forward), padded(decay_reverse)

    joined = to_scan(ssm_input, input_map, output_map)
    keys_at, queries_at = width, width + maps

    ahead = Scan((ssm_input, 0), (input_map, 0), (output_map, 0), decay_f, width, False)
    ahead_in = carried(ahead.states(), forward_factors, False)
    ahead.inner()
    y_forward = ahead.finish(ahead_in)

    behind = Scan((joined, 0), (joined, keys_at), (joined, queries_at), decay_r, width, True)
    behind_in = carried(behind.states(), reverse_factors, True)
    behind.inner()
    y_reverse = to_raster(behind.finish(behind_in))

    skip_cols = jnp.repeat(skip_gain, HEAD_DIM)
    combined = (
        y_forward.astype(F32) + y_reverse.astype(F32) + skip_cols * ssm_input.astype(F32)
    )
    scaled_grad = norm_gain * grad_normed.astype(F32)
    both = jnp.stack(
        [jnp.sum(combined * combined, axis=1), jnp.sum(combined * scaled_grad, axis=1)]
    )
    squares, inner_sum = lax.psum(both, "head")
    inv_rms = lax.rsqrt(squares / FEATURES + EPSILON)
    normed_output = (combined * inv_rms[:, None] * norm_gain).astype(BF16)
    grad_combined = (
        inv_rms[:, None] * scaled_grad - combined * (inv_rms**3 * inner_sum / FEATURES)[:, None]
    ).astype(BF16)

    grad_scan = to_scan(grad_combined)
    ahead_grad = Scan((grad_combined, 0), (output_map, 0), (input_map, 0), decay_f, width, True)
    ahead_grad_in = carried(ahead_grad.states(), forward_factors, True)
    ahead_grad.inner()
    grad_forward = ahead_grad.finish(ahead_grad_in)

    behind_grad = Scan((grad_scan, 0), (joined, queries_at), (joined, keys_at), decay_r, width, False)
    behind_grad_in = carried(behind_grad.states(), reverse_factors, False)
    behind_grad.inner()
    grad_reverse = to_raster(behind_grad.finish(behind_grad_in))

    grad_input = (
        grad_forward.astype(F32)
        + grad_reverse.astype(F32)
        + skip_cols * grad_combined.astype(F32)
    )
    return (normed_output, grad_input.astype(BF16))


def solution(mesh):
    return jax.shard_map(
        shards,
        mesh=mesh,
        in_specs=(
            P("seq", "head"),
            P("seq", "head"),
            P("seq", "head"),
            P("head", "seq"),
            P("head", "seq"),
            P("head"),
            P("head"),
            P("seq"),
            P("seq"),
            P("seq", "head"),
        ),
        out_specs=(P("seq", "head"), P("seq", "head")),
        check_vma=False,
    )
```

```python
import functools

import jax
import jax.numpy as jnp
from jax import lax
from jax.experimental import pallas as pl
from jax.experimental.pallas import tpu as pltpu
from jax.sharding import PartitionSpec as P

HEAD_DIM = 64
STATE = 128
SPAN = 256
FEATURES = 3072
PAD = 8
LANES = 128
EPSILON = 1e-05
F32 = jnp.float32
BF16 = jnp.bfloat16


def triangle(lower):
    rows = lax.broadcasted_iota(jnp.int32, (SPAN, SPAN), 0)
    cols = lax.broadcasted_iota(jnp.int32, (SPAN, SPAN), 1)
    return cols <= rows if lower else cols >= rows


def spread_pair(columns, pair):
    shape = (columns.shape[0], LANES)
    lane = lax.broadcasted_iota(jnp.int32, shape, 1)
    return jnp.where(
        lane < HEAD_DIM, columns[:, 2 * pair : 2 * pair + 1], columns[:, 2 * pair + 1 : 2 * pair + 2]
    )


def spread_heads(columns, pairs):
    return jnp.concatenate([spread_pair(columns, pair) for pair in range(pairs)], axis=1)


def running_columns(decay):
    ones = jnp.where(triangle(True), 1.0, 0.0).astype(BF16)
    return lax.dot_general(ones, decay, (((1,), (1,)), ((), ())), preferred_element_type=F32)


def running_rows(decay):
    ones = jnp.where(triangle(False), 1.0, 0.0).astype(BF16)
    return jnp.dot(decay, ones, preferred_element_type=F32)


def states_kernel(reverse, spans, v_ref, k_ref, decay_ref, before_ref, total_ref):
    pairs = v_ref.shape[1] // LANES
    order = range(spans)
    run = None
    for span in order[::-1] if reverse else order:
        rows = slice(span * SPAN, (span + 1) * SPAN)
        cum = running_columns(decay_ref[0, :, rows].astype(BF16))
        end = cum[SPAN - 1 : SPAN]
        weight = jnp.exp(cum) if reverse else jnp.exp(end - cum)
        scaled = (v_ref[rows, :].astype(F32) * spread_heads(weight, pairs)).astype(BF16)
        state = lax.dot_general(
            k_ref[rows, :], scaled, (((0,), (0,)), ((), ())), preferred_element_type=F32
        )
        if run is None:
            before_ref[span] = jnp.zeros_like(state)
            run = state
        else:
            before_ref[span] = run
            run = run * spread_heads(jnp.exp(end), pairs) + state
    total_ref[...] = run.astype(BF16)


def inner_kernel(reverse, spans, v_ref, k_ref, q_ref, decay_ref, out_ref):
    pairs = v_ref.shape[1] // LANES
    allowed = triangle(not reverse)
    lane = lax.broadcasted_iota(jnp.int32, (SPAN, LANES), 1)
    for span in range(spans):
        rows = slice(span * SPAN, (span + 1) * SPAN)
        decay = decay_ref[0, :, rows].astype(BF16)
        cum_col = running_columns(decay)
        cum_row = running_rows(decay)
        scores = lax.dot_general(
            q_ref[rows, :], k_ref[rows, :], (((1,), (1,)), ((), ())), preferred_element_type=F32
        )
        scores = jnp.where(allowed, scores, 0.0)
        for pair in range(pairs):
            values = v_ref[rows, pair * LANES : (pair + 1) * LANES]
            parts = []
            for head in (2 * pair, 2 * pair + 1):
                col, row = cum_col[:, head : head + 1], cum_row[head : head + 1, :]
                gap = row - col if reverse else col - row
                weights = (scores * jnp.exp(jnp.minimum(gap, 0.0))).astype(BF16)
                parts.append(jnp.dot(weights, values, preferred_element_type=F32))
            out_ref[rows, pair * LANES : (pair + 1) * LANES] = jnp.where(
                lane < HEAD_DIM, parts[0], parts[1]
            )


def finish_kernel(reverse, spans, inner_ref, q_ref, decay_ref, before_ref, incoming_ref, out_ref):
    pairs = inner_ref.shape[1] // LANES
    order = range(spans)
    incoming = incoming_ref[...].astype(F32)
    passed = None
    for span in order[::-1] if reverse else order:
        rows = slice(span * SPAN, (span + 1) * SPAN)
        cum = running_columns(decay_ref[0, :, rows].astype(BF16))
        end = cum[SPAN - 1 : SPAN]
        weight = jnp.exp(end - cum) if reverse else jnp.exp(cum)
        if passed is None:
            entering = incoming
            passed = end
        else:
            entering = before_ref[span] + incoming * spread_heads(jnp.exp(passed), pairs)
            passed = passed + end
        outer = jnp.dot(q_ref[rows, :], entering.astype(BF16), preferred_element_type=F32)
        out_ref[rows, :] = (inner_ref[rows, :] + outer * spread_heads(weight, pairs)).astype(BF16)


class Scan:
    def __init__(self, values, keys, queries, decay, width, reverse):
        self.decay, self.reverse, self.width = decay, reverse, width
        self.groups = decay.shape[0]
        self.tokens = decay.shape[2]
        self.spans = self.tokens // SPAN
        self.cols = width // self.groups
        self.values, self.keys, self.queries = values, keys, queries

    def cut(self, operand, size):
        array, first = operand
        base = first // size
        return array, pl.BlockSpec((self.tokens, size), lambda g: (0, base + g))

    def call(self, body, operands, outs, out_specs, flops):
        arrays, specs = zip(*operands)
        shapes = jax.tree.leaves(outs)
        moved = sum(s.size * s.dtype.itemsize for s in shapes) * 2
        return pl.pallas_call(
            functools.partial(body, self.reverse, self.spans),
            grid=(self.groups,),
            in_specs=list(specs),
            out_specs=out_specs,
            out_shape=outs,
            compiler_params=pltpu.CompilerParams(vmem_limit_bytes=48 * 2**20),
            cost_estimate=pl.CostEstimate(flops=flops, bytes_accessed=moved, transcendentals=0),
        )(*arrays)

    def decay_cut(self):
        return self.decay, pl.BlockSpec((1, PAD, self.tokens), lambda g: (g, 0, 0))

    def states(self):
        wide = pl.BlockSpec((STATE, self.cols), lambda g: (0, g))
        deep = pl.BlockSpec((self.spans, STATE, self.cols), lambda g: (0, 0, g))
        self.before, total = self.call(
            states_kernel,
            [self.cut(self.values, self.cols), self.cut(self.keys, STATE), self.decay_cut()],
            (
                jax.ShapeDtypeStruct((self.spans, STATE, self.width), F32),
                jax.ShapeDtypeStruct((STATE, self.width), BF16),
            ),
            (deep, wide),
            2 * self.tokens * STATE * self.width,
        )
        return total

    def inner(self):
        self.near = self.call(
            inner_kernel,
            [
                self.cut(self.values, self.cols),
                self.cut(self.keys, STATE),
                self.cut(self.queries, STATE),
                self.decay_cut(),
            ],
            jax.ShapeDtypeStruct((self.tokens, self.width), F32),
            pl.BlockSpec((self.tokens, self.cols), lambda g: (0, g)),
            8 * self.tokens * SPAN * self.width,
        )

    def finish(self, incoming, first):
        base = first // self.cols
        wide = pl.BlockSpec((STATE, self.cols), lambda g: (0, base + g))
        deep = pl.BlockSpec((self.spans, STATE, self.cols), lambda g: (0, 0, g))
        rows = pl.BlockSpec((self.tokens, self.cols), lambda g: (0, g))
        return self.call(
            finish_kernel,
            [
                (self.near, rows),
                self.cut(self.queries, STATE),
                self.decay_cut(),
                (self.before, deep),
                (incoming, wide),
            ],
            jax.ShapeDtypeStruct((self.tokens, self.width), BF16),
            rows,
            2 * self.tokens * STATE * self.width,
        )


def prefix_kernel(directions, arrived_ref, factor_ref, out_ref):
    count, rows, width = arrived_ref.shape
    width //= len(directions)
    for place, reverse in enumerate(directions):
        cols = slice(place * width, (place + 1) * width)
        run = jnp.zeros((rows, width), F32)
        order = range(count)
        for index in order[::-1] if reverse else order:
            out_ref[index, :, cols] = run.astype(BF16)
            run = run * factor_ref[index, :, cols] + arrived_ref[index, :, cols].astype(F32)


def carried(totals, factors, directions):
    count = lax.axis_size("seq")
    total = jnp.concatenate(totals, axis=1)
    pieces = total.reshape(count, STATE // count, -1)
    arrived = lax.all_to_all(pieces, "seq", split_axis=0, concat_axis=0, tiled=True)
    composed = pl.pallas_call(
        functools.partial(prefix_kernel, directions),
        out_shape=jax.ShapeDtypeStruct(arrived.shape, BF16),
    )(arrived, factors)
    back = lax.all_to_all(composed, "seq", split_axis=0, concat_axis=0, tiled=True)
    return back.reshape(total.shape)


def gather_kernel(counts, index_ref, *refs):
    sources, out_ref = refs[: len(counts)], refs[-1]

    @pl.loop(0, out_ref.shape[0])
    def _(unit):
        first = 0
        for source, width in zip(sources, counts):
            out_ref[unit, :, first : first + width] = source[index_ref[unit]]
            first += width


def gathered(arrays, index):
    widths = tuple(array.shape[2] for array in arrays)
    units, rows = arrays[0].shape[:2]
    whole = pl.BlockSpec(memory_space=pltpu.VMEM)
    return pl.pallas_call(
        functools.partial(gather_kernel, widths),
        in_specs=[pl.BlockSpec(memory_space=pltpu.SMEM)] + [whole] * len(arrays),
        out_specs=whole,
        out_shape=jax.ShapeDtypeStruct((units, rows, sum(widths)), arrays[0].dtype),
        compiler_params=pltpu.CompilerParams(vmem_limit_bytes=48 * 2**20),
    )(index, *arrays)


def inverse(order):
    count = order.shape[0]
    spots = jnp.arange(count, dtype=jnp.int32)
    return jnp.sum(jnp.where(order[None, :] == spots[:, None], spots[None, :], 0), axis=1)


def shards(
    ssm_input,
    input_map,
    output_map,
    decay_forward,
    decay_reverse,
    skip_gain,
    norm_gain,
    scan_order,
    raster_order,
    grad_normed,
):
    unit_count = scan_order.shape[0]
    tok_rows, width = ssm_input.shape
    unit_rows = tok_rows // unit_count
    maps = input_map.shape[1]
    groups = maps // STATE
    heads = decay_forward.shape[0]
    raster_dest = raster_order // unit_count
    scan_source = scan_order // unit_count
    send_scan = inverse(raster_dest)
    send_raster = inverse(scan_source)

    def units(array):
        return array.reshape(unit_count, unit_rows, -1)

    def sent(arrays, send_index):
        outgoing = gathered([units(array) for array in arrays], send_index)
        return lax.all_to_all(outgoing, "seq", split_axis=0, concat_axis=0, tiled=True)

    def placed(arrived, recv_index):
        return gathered([arrived], recv_index).reshape(tok_rows, -1)

    def padded(decay):
        wide = decay.astype(F32).reshape(groups, heads // groups, tok_rows)
        return jnp.pad(wide, ((0, 0), (0, PAD - heads // groups), (0, 0)))

    sums = jnp.stack([decay_forward, decay_reverse]).astype(F32).sum(axis=2)
    copies = jnp.broadcast_to(sums[None], (lax.axis_size("seq"), *sums.shape))
    all_sums = lax.all_to_all(copies, "seq", split_axis=0, concat_axis=0, tiled=True)
    factors = jnp.repeat(jnp.exp(all_sums), HEAD_DIM, axis=2)
    factors = factors.reshape(factors.shape[0], 1, 2 * width)
    decay_f, decay_r = padded(decay_forward), padded(decay_reverse)

    keys_at, queries_at = width, width + maps

    arrived = sent([ssm_input, input_map, output_map], send_scan)
    ahead = Scan((ssm_input, 0), (input_map, 0), (output_map, 0), decay_f, width, False)
    ahead_total = ahead.states()
    ahead.inner()
    arrived, ahead_total, ahead.near, factors = lax.optimization_barrier(
        (arrived, ahead_total, ahead.near, factors)
    )
    joined = placed(arrived, scan_source)
    behind = Scan((joined, 0), (joined, keys_at), (joined, queries_at), decay_r, width, True)
    entering = carried((ahead_total, behind.states()), factors, (False, True))
    behind.inner()
    y_reverse_sent = sent([behind.finish(entering, width)], send_raster)
    y_forward = ahead.finish(entering, 0)
    y_reverse = placed(y_reverse_sent, raster_dest)

    skip_cols = jnp.repeat(skip_gain, HEAD_DIM)
    combined = (
        y_forward.astype(F32) + y_reverse.astype(F32) + skip_cols * ssm_input.astype(F32)
    )
    scaled_grad = norm_gain * grad_normed.astype(F32)
    both = jnp.stack(
        [jnp.sum(combined * combined, axis=1), jnp.sum(combined * scaled_grad, axis=1)]
    )
    squares, inner_sum = lax.psum(both, "head")
    inv_rms = lax.rsqrt(squares / FEATURES + EPSILON)
    normed_output = (combined * inv_rms[:, None] * norm_gain).astype(BF16)
    grad_combined = (
        inv_rms[:, None] * scaled_grad - combined * (inv_rms**3 * inner_sum / FEATURES)[:, None]
    ).astype(BF16)

    arrived = sent([grad_combined], send_scan)
    ahead_grad = Scan((grad_combined, 0), (output_map, 0), (input_map, 0), decay_f, width, True)
    ahead_total = ahead_grad.states()
    ahead_grad.inner()
    arrived, ahead_total, ahead_grad.near = lax.optimization_barrier(
        (arrived, ahead_total, ahead_grad.near)
    )
    grad_scan = placed(arrived, scan_source)
    behind_grad = Scan((grad_scan, 0), (joined, queries_at), (joined, keys_at), decay_r, width, False)
    entering = carried((ahead_total, behind_grad.states()), factors, (True, False))
    behind_grad.inner()
    grad_reverse_sent = sent([behind_grad.finish(entering, width)], send_raster)
    grad_forward = ahead_grad.finish(entering, 0)
    grad_reverse = placed(grad_reverse_sent, raster_dest)

    grad_input = (
        grad_forward.astype(F32)
        + grad_reverse.astype(F32)
        + skip_cols * grad_combined.astype(F32)
    )
    return (normed_output, grad_input.astype(BF16))


def solution(mesh):
    return jax.shard_map(
        shards,
        mesh=mesh,
        in_specs=(
            P("seq", "head"),
            P("seq", "head"),
            P("seq", "head"),
            P("head", "seq"),
            P("head", "seq"),
            P("head"),
            P("head"),
            P("seq"),
            P("seq"),
            P("seq", "head"),
        ),
        out_specs=(P("seq", "head"), P("seq", "head")),
        check_vma=False,
    )
```

```python
import functools

import jax
import jax.numpy as jnp
from jax import lax
from jax.experimental import pallas as pl
from jax.experimental.pallas import tpu as pltpu
from jax.sharding import PartitionSpec as P

HEAD_DIM = 64
STATE = 128
SPAN = 256
FEATURES = 3072
PAD = 8
LANES = 128
EPSILON = 1e-05
F32 = jnp.float32
BF16 = jnp.bfloat16


def triangle(lower):
    rows = lax.broadcasted_iota(jnp.int32, (SPAN, SPAN), 0)
    cols = lax.broadcasted_iota(jnp.int32, (SPAN, SPAN), 1)
    return cols <= rows if lower else cols >= rows


def spread_pair(columns, pair):
    shape = (columns.shape[0], LANES)
    lane = lax.broadcasted_iota(jnp.int32, shape, 1)
    return jnp.where(
        lane < HEAD_DIM, columns[:, 2 * pair : 2 * pair + 1], columns[:, 2 * pair + 1 : 2 * pair + 2]
    )


def spread_heads(columns, pairs):
    return jnp.concatenate([spread_pair(columns, pair) for pair in range(pairs)], axis=1)


def running_columns(decay):
    ones = jnp.where(triangle(True), 1.0, 0.0).astype(BF16)
    return lax.dot_general(ones, decay, (((1,), (1,)), ((), ())), preferred_element_type=F32)


def running_rows(decay):
    ones = jnp.where(triangle(False), 1.0, 0.0).astype(BF16)
    return jnp.dot(decay, ones, preferred_element_type=F32)


def states_kernel(reverse, spans, v_ref, k_ref, decay_ref, before_ref, total_ref):
    pairs = v_ref.shape[1] // LANES
    order = range(spans)
    run = None
    for span in order[::-1] if reverse else order:
        rows = slice(span * SPAN, (span + 1) * SPAN)
        cum = running_columns(decay_ref[0, :, rows].astype(BF16))
        end = cum[SPAN - 1 : SPAN]
        weight = jnp.exp(cum) if reverse else jnp.exp(end - cum)
        scaled = (v_ref[rows, :].astype(F32) * spread_heads(weight, pairs)).astype(BF16)
        state = lax.dot_general(
            k_ref[rows, :], scaled, (((0,), (0,)), ((), ())), preferred_element_type=F32
        )
        if run is None:
            before_ref[span] = jnp.zeros_like(state)
            run = state
        else:
            before_ref[span] = run
            run = run * spread_heads(jnp.exp(end), pairs) + state
    total_ref[...] = run.astype(BF16)


def inner_kernel(reverse, spans, v_ref, k_ref, q_ref, decay_ref, out_ref):
    pairs = v_ref.shape[1] // LANES
    allowed = triangle(not reverse)
    lane = lax.broadcasted_iota(jnp.int32, (SPAN, LANES), 1)
    for span in range(spans):
        rows = slice(span * SPAN, (span + 1) * SPAN)
        decay = decay_ref[0, :, rows].astype(BF16)
        cum_col = running_columns(decay)
        cum_row = running_rows(decay)
        scores = lax.dot_general(
            q_ref[rows, :], k_ref[rows, :], (((1,), (1,)), ((), ())), preferred_element_type=F32
        )
        scores = jnp.where(allowed, scores, 0.0)
        for pair in range(pairs):
            values = v_ref[rows, pair * LANES : (pair + 1) * LANES]
            parts = []
            for head in (2 * pair, 2 * pair + 1):
                col, row = cum_col[:, head : head + 1], cum_row[head : head + 1, :]
                gap = row - col if reverse else col - row
                weights = (scores * jnp.exp(jnp.minimum(gap, 0.0))).astype(BF16)
                parts.append(jnp.dot(weights, values, preferred_element_type=F32))
            out_ref[rows, pair * LANES : (pair + 1) * LANES] = jnp.where(
                lane < HEAD_DIM, parts[0], parts[1]
            )


def finish_kernel(reverse, spans, inner_ref, q_ref, decay_ref, before_ref, incoming_ref, out_ref, slot_ref=None):
    pairs = inner_ref.shape[1] // LANES
    order = range(spans)
    incoming = incoming_ref[...].astype(F32)
    passed = None
    for span in order[::-1] if reverse else order:
        rows = slice(span * SPAN, (span + 1) * SPAN)
        cum = running_columns(decay_ref[0, :, rows].astype(BF16))
        end = cum[SPAN - 1 : SPAN]
        weight = jnp.exp(end - cum) if reverse else jnp.exp(cum)
        if passed is None:
            entering = incoming
            passed = end
        else:
            entering = before_ref[span] + incoming * spread_heads(jnp.exp(passed), pairs)
            passed = passed + end
        outer = jnp.dot(q_ref[rows, :], entering.astype(BF16), preferred_element_type=F32)
        total = inner_ref[rows, :] + outer * spread_heads(weight, pairs)
        if slot_ref is None:
            out_ref[rows, :] = total.astype(BF16)
            continue
        unit_rows = out_ref.shape[1]
        per_span = SPAN // unit_rows
        for unit in range(per_span):
            piece = total[unit * unit_rows : (unit + 1) * unit_rows]
            out_ref[slot_ref[span * per_span + unit]] = piece.astype(BF16)


class Scan:
    def __init__(self, values, keys, queries, decay, width, reverse):
        self.decay, self.reverse, self.width = decay, reverse, width
        self.groups = decay.shape[0]
        self.tokens = decay.shape[2]
        self.spans = self.tokens // SPAN
        self.cols = width // self.groups
        self.values, self.keys, self.queries = values, keys, queries

    def cut(self, operand, size):
        array, first = operand
        lead = (slice(None),) * (array.ndim - 1)

        def view(ref, group):
            at = pl.multiple_of(first + group * size, LANES)
            return ref.at[(*lead, pl.ds(at, size))]

        return array, view

    def decay_cut(self):
        return self.decay, lambda ref, group: ref.at[pl.ds(group, 1)]

    def call(self, body, operands, outs, flops, slots=None):
        arrays = []
        for array, _ in operands:
            if not any(array is other for other in arrays):
                arrays.append(array)
        places = [next(i for i, other in enumerate(arrays) if other is a) for a, _ in operands]
        out_views = [self.cut((out, 0), out.shape[-1] // self.groups)[1] for out in outs]

        def kernel(*refs):
            ins, results = refs[: len(arrays)], refs[len(refs) - len(outs) :]

            @pl.loop(0, self.groups)
            def _(group):
                taken = [view(ins[place], group) for place, (_, view) in zip(places, operands)]
                given = [view(ref, group) for ref, view in zip(results, out_views)]
                extra = () if slots is None else (refs[len(arrays)],)
                body(self.reverse, self.spans, *taken, *given, *extra)

        whole = pl.BlockSpec(memory_space=pltpu.VMEM)
        index = [] if slots is None else [slots]
        return pl.pallas_call(
            kernel,
            in_specs=[whole] * len(arrays) + [pl.BlockSpec(memory_space=pltpu.SMEM)] * len(index),
            out_specs=[whole] * len(outs),
            out_shape=outs,
            compiler_params=pltpu.CompilerParams(vmem_limit_bytes=48 * 2**20),
            cost_estimate=pl.CostEstimate(
                flops=flops, bytes_accessed=2**22, transcendentals=0
            ),
        )(*arrays, *index)

    def states(self):
        self.before, total = self.call(
            states_kernel,
            [self.cut(self.values, self.cols), self.cut(self.keys, STATE), self.decay_cut()],
            [
                jax.ShapeDtypeStruct((self.spans, STATE, self.width), F32),
                jax.ShapeDtypeStruct((STATE, self.width), BF16),
            ],
            2 * self.tokens * STATE * self.width,
        )
        return total

    def inner(self):
        (self.near,) = self.call(
            inner_kernel,
            [
                self.cut(self.values, self.cols),
                self.cut(self.keys, STATE),
                self.cut(self.queries, STATE),
                self.decay_cut(),
            ],
            [jax.ShapeDtypeStruct((self.tokens, self.width), F32)],
            8 * self.tokens * SPAN * self.width,
        )

    def finish(self, incoming, first, slots=None):
        shape = (self.tokens, self.width)
        if slots is not None:
            shape = (slots.shape[0], self.tokens // slots.shape[0], self.width)
        (result,) = self.call(
            finish_kernel,
            [
                self.cut((self.near, 0), self.cols),
                self.cut(self.queries, STATE),
                self.decay_cut(),
                self.cut((self.before, 0), self.cols),
                self.cut((incoming, first), self.cols),
            ],
            [jax.ShapeDtypeStruct(shape, BF16)],
            2 * self.tokens * STATE * self.width,
            slots,
        )
        return result


def prefix_kernel(directions, arrived_ref, factor_ref, out_ref):
    count, rows, width = arrived_ref.shape
    width //= len(directions)
    for place, reverse in enumerate(directions):
        cols = slice(place * width, (place + 1) * width)
        run = jnp.zeros((rows, width), F32)
        order = range(count)
        for index in order[::-1] if reverse else order:
            out_ref[index, :, cols] = run.astype(BF16)
            run = run * factor_ref[index, :, cols] + arrived_ref[index, :, cols].astype(F32)


def carried(totals, factors, directions, sums=None):
    count = lax.axis_size("seq")
    total = jnp.concatenate(totals, axis=1)
    pieces = total.reshape(count, STATE // count, -1)
    if sums is not None:
        parts, rest = [], sums.reshape(-1)
        for _ in range(3):
            parts.append(lax.reduce_precision(rest, 8, 7))
            rest = rest - parts[-1]
        taken = sums.size
        row = jnp.concatenate(parts).astype(BF16)
        row = jnp.pad(row, (0, -row.size % LANES))
        row = jnp.broadcast_to(row, (*pieces.shape[:2], row.size))
        pieces = jnp.concatenate([pieces, row], axis=2)
    arrived = lax.all_to_all(pieces, "seq", split_axis=0, concat_axis=0, tiled=True)
    if sums is not None:
        width = total.shape[1]
        rows = arrived[:, 0, width : width + 3 * taken].astype(F32).reshape(count, 3, taken)
        factors = jnp.exp(jnp.sum(rows, axis=1))[:, :, None]
        factors = jnp.broadcast_to(factors, (count, taken, HEAD_DIM)).reshape(count, 1, width)
        arrived = arrived[:, :, :width]
    composed = pl.pallas_call(
        functools.partial(prefix_kernel, directions),
        out_shape=jax.ShapeDtypeStruct(arrived.shape, BF16),
    )(arrived, factors)
    back = lax.all_to_all(composed, "seq", split_axis=0, concat_axis=0, tiled=True)
    return back.reshape(total.shape), factors


def gather_kernel(counts, index_ref, *refs):
    sources, out_ref = refs[: len(counts)], refs[-1]

    @pl.loop(0, out_ref.shape[0])
    def _(unit):
        first = 0
        for source, width in zip(sources, counts):
            out_ref[unit, :, first : first + width] = source[index_ref[unit]]
            first += width


def gathered(arrays, index):
    widths = tuple(array.shape[2] for array in arrays)
    units, rows = arrays[0].shape[:2]
    whole = pl.BlockSpec(memory_space=pltpu.VMEM)
    return pl.pallas_call(
        functools.partial(gather_kernel, widths),
        in_specs=[pl.BlockSpec(memory_space=pltpu.SMEM)] + [whole] * len(arrays),
        out_specs=whole,
        out_shape=jax.ShapeDtypeStruct((units, rows, sum(widths)), arrays[0].dtype),
        compiler_params=pltpu.CompilerParams(vmem_limit_bytes=48 * 2**20),
    )(index, *arrays)


def inverse(order):
    count = order.shape[0]
    spots = jnp.arange(count, dtype=jnp.int32)
    return jnp.sum(jnp.where(order[None, :] == spots[:, None], spots[None, :], 0), axis=1)


def shards(
    ssm_input,
    input_map,
    output_map,
    decay_forward,
    decay_reverse,
    skip_gain,
    norm_gain,
    scan_order,
    raster_order,
    grad_normed,
):
    unit_count = scan_order.shape[0]
    tok_rows, width = ssm_input.shape
    unit_rows = tok_rows // unit_count
    maps = input_map.shape[1]
    groups = maps // STATE
    heads = decay_forward.shape[0]
    raster_dest = raster_order // unit_count
    scan_source = scan_order // unit_count
    send_scan = inverse(raster_dest)

    def units(array):
        return array.reshape(unit_count, unit_rows, -1)

    def swapped(outgoing):
        return lax.all_to_all(outgoing, "seq", split_axis=0, concat_axis=0, tiled=True)

    def sent(arrays, send_index):
        return swapped(gathered([units(array) for array in arrays], send_index))

    def placed(arrived, recv_index):
        return gathered([arrived], recv_index).reshape(tok_rows, -1)

    def padded(decay):
        wide = decay.astype(F32).reshape(groups, heads // groups, tok_rows)
        return jnp.pad(wide, ((0, 0), (0, PAD - heads // groups), (0, 0)))

    sums = jnp.stack([decay_forward, decay_reverse]).astype(F32).sum(axis=2)
    decay_f, decay_r = padded(decay_forward), padded(decay_reverse)

    keys_at, queries_at = width, width + maps

    arrived = sent([ssm_input, input_map, output_map], send_scan)
    ahead = Scan((ssm_input, 0), (input_map, 0), (output_map, 0), decay_f, width, False)
    ahead_total = ahead.states()
    ahead.inner()
    arrived, ahead_total, ahead.near, sums = lax.optimization_barrier(
        (arrived, ahead_total, ahead.near, sums)
    )
    joined = placed(arrived, scan_source)
    behind = Scan((joined, 0), (joined, keys_at), (joined, queries_at), decay_r, width, True)
    entering, factors = carried((ahead_total, behind.states()), None, (False, True), sums)
    behind.inner()
    y_reverse_sent = swapped(behind.finish(entering, width, scan_source))
    y_forward = ahead.finish(entering, 0)
    y_reverse = placed(y_reverse_sent, raster_dest)

    skip_cols = jnp.repeat(skip_gain, HEAD_DIM)
    combined = (
        y_forward.astype(F32) + y_reverse.astype(F32) + skip_cols * ssm_input.astype(F32)
    )
    scaled_grad = norm_gain * grad_normed.astype(F32)
    both = jnp.stack(
        [jnp.sum(combined * combined, axis=1), jnp.sum(combined * scaled_grad, axis=1)]
    )
    squares, inner_sum = lax.psum(both, "head")
    inv_rms = lax.rsqrt(squares / FEATURES + EPSILON)
    normed_output = (combined * inv_rms[:, None] * norm_gain).astype(BF16)
    grad_combined = (
        inv_rms[:, None] * scaled_grad - combined * (inv_rms**3 * inner_sum / FEATURES)[:, None]
    ).astype(BF16)

    arrived = sent([grad_combined], send_scan)
    ahead_grad = Scan((grad_combined, 0), (output_map, 0), (input_map, 0), decay_f, width, True)
    ahead_total = ahead_grad.states()
    ahead_grad.inner()
    arrived, ahead_total, ahead_grad.near = lax.optimization_barrier(
        (arrived, ahead_total, ahead_grad.near)
    )
    grad_scan = placed(arrived, scan_source)
    behind_grad = Scan((grad_scan, 0), (joined, queries_at), (joined, keys_at), decay_r, width, False)
    entering, _ = carried((ahead_total, behind_grad.states()), factors, (True, False))
    behind_grad.inner()
    grad_reverse_sent = swapped(behind_grad.finish(entering, width, scan_source))
    grad_forward = ahead_grad.finish(entering, 0)
    grad_reverse = placed(grad_reverse_sent, raster_dest)

    grad_input = (
        grad_forward.astype(F32)
        + grad_reverse.astype(F32)
        + skip_cols * grad_combined.astype(F32)
    )
    return (normed_output, grad_input.astype(BF16))


def solution(mesh):
    return jax.shard_map(
        shards,
        mesh=mesh,
        in_specs=(
            P("seq", "head"),
            P("seq", "head"),
            P("seq", "head"),
            P("head", "seq"),
            P("head", "seq"),
            P("head"),
            P("head"),
            P("seq"),
            P("seq"),
            P("seq", "head"),
        ),
        out_specs=(P("seq", "head"), P("seq", "head")),
        check_vma=False,
    )
```

```python
import functools

import jax
import jax.numpy as jnp
from jax import lax
from jax.experimental import pallas as pl
from jax.experimental.pallas import tpu as pltpu
from jax.sharding import PartitionSpec as P

HEAD_DIM = 64
STATE = 128
SPAN = 256
FEATURES = 3072
PAD = 8
LANES = 128
EPSILON = 1e-05
F32 = jnp.float32
BF16 = jnp.bfloat16


def triangle(lower):
    rows = lax.broadcasted_iota(jnp.int32, (SPAN, SPAN), 0)
    cols = lax.broadcasted_iota(jnp.int32, (SPAN, SPAN), 1)
    return cols <= rows if lower else cols >= rows


def spread_pair(columns, pair):
    shape = (columns.shape[0], LANES)
    lane = lax.broadcasted_iota(jnp.int32, shape, 1)
    return jnp.where(
        lane < HEAD_DIM, columns[:, 2 * pair : 2 * pair + 1], columns[:, 2 * pair + 1 : 2 * pair + 2]
    )


def spread_heads(columns, pairs):
    return jnp.concatenate([spread_pair(columns, pair) for pair in range(pairs)], axis=1)


def running_columns(decay):
    ones = jnp.where(triangle(True), 1.0, 0.0).astype(BF16)
    return lax.dot_general(ones, decay, (((1,), (1,)), ((), ())), preferred_element_type=F32)


def running_rows(decay):
    ones = jnp.where(triangle(False), 1.0, 0.0).astype(BF16)
    return jnp.dot(decay, ones, preferred_element_type=F32)


def states_kernel(reverse, spans, v_ref, k_ref, decay_ref, before_ref, total_ref):
    pairs = v_ref.shape[1] // LANES
    order = range(spans)
    run = None
    for span in order[::-1] if reverse else order:
        rows = slice(span * SPAN, (span + 1) * SPAN)
        cum = running_columns(decay_ref[0, :, rows].astype(BF16))
        end = cum[SPAN - 1 : SPAN]
        weight = jnp.exp(cum) if reverse else jnp.exp(end - cum)
        scaled = (v_ref[rows, :].astype(F32) * spread_heads(weight, pairs)).astype(BF16)
        state = lax.dot_general(
            k_ref[rows, :], scaled, (((0,), (0,)), ((), ())), preferred_element_type=F32
        )
        if run is None:
            run = state
        else:
            before_ref[span if reverse else span - 1] = run
            run = run * spread_heads(jnp.exp(end), pairs) + state
    total_ref[...] = run.astype(BF16)


def inner_kernel(reverse, spans, v_ref, k_ref, q_ref, decay_ref, out_ref):
    pairs = v_ref.shape[1] // LANES
    allowed = triangle(not reverse)
    lane = lax.broadcasted_iota(jnp.int32, (SPAN, LANES), 1)
    for span in range(spans):
        rows = slice(span * SPAN, (span + 1) * SPAN)
        decay = decay_ref[0, :, rows].astype(BF16)
        cum_col = running_columns(decay)
        cum_row = running_rows(decay)
        scores = lax.dot_general(
            q_ref[rows, :], k_ref[rows, :], (((1,), (1,)), ((), ())), preferred_element_type=F32
        )
        scores = jnp.where(allowed, scores, 0.0)
        for pair in range(pairs):
            values = v_ref[rows, pair * LANES : (pair + 1) * LANES]
            parts = []
            for head in (2 * pair, 2 * pair + 1):
                col, row = cum_col[:, head : head + 1], cum_row[head : head + 1, :]
                gap = row - col if reverse else col - row
                weights = (scores * jnp.exp(jnp.minimum(gap, 0.0))).astype(BF16)
                parts.append(jnp.dot(weights, values, preferred_element_type=F32))
            out_ref[rows, pair * LANES : (pair + 1) * LANES] = jnp.where(
                lane < HEAD_DIM, parts[0], parts[1]
            ).astype(BF16)


def finish_kernel(reverse, spans, inner_ref, q_ref, decay_ref, before_ref, incoming_ref, out_ref, slot_ref=None):
    pairs = inner_ref.shape[1] // LANES
    order = range(spans)
    incoming = incoming_ref[...].astype(F32)
    passed = None
    for span in order[::-1] if reverse else order:
        rows = slice(span * SPAN, (span + 1) * SPAN)
        cum = running_columns(decay_ref[0, :, rows].astype(BF16))
        end = cum[SPAN - 1 : SPAN]
        weight = jnp.exp(end - cum) if reverse else jnp.exp(cum)
        if passed is None:
            entering = incoming
            passed = end
        else:
            entering = before_ref[span if reverse else span - 1] + incoming * spread_heads(jnp.exp(passed), pairs)
            passed = passed + end
        outer = jnp.dot(q_ref[rows, :], entering.astype(BF16), preferred_element_type=F32)
        total = inner_ref[rows, :].astype(F32) + outer * spread_heads(weight, pairs)
        if slot_ref is None:
            out_ref[rows, :] = total.astype(BF16)
            continue
        unit_rows = out_ref.shape[1]
        per_span = SPAN // unit_rows
        for unit in range(per_span):
            piece = total[unit * unit_rows : (unit + 1) * unit_rows]
            out_ref[slot_ref[span * per_span + unit]] = piece.astype(BF16)


class Scan:
    def __init__(self, values, keys, queries, decay, width, reverse):
        self.decay, self.reverse, self.width = decay, reverse, width
        self.groups = decay.shape[0]
        self.tokens = decay.shape[2]
        self.spans = self.tokens // SPAN
        self.cols = width // self.groups
        self.values, self.keys, self.queries = values, keys, queries

    def cut(self, operand, size):
        array, first = operand
        lead = (slice(None),) * (array.ndim - 1)

        def view(ref, group):
            at = first + group * size
            return ref.at[(*lead, pl.ds(at, size))]

        return array, view

    def decay_cut(self):
        return self.decay, lambda ref, group: ref.at[pl.ds(group, 1)]

    def call(self, body, operands, outs, flops, slots=None):
        arrays = []
        for array, _ in operands:
            if not any(array is other for other in arrays):
                arrays.append(array)
        places = [next(i for i, other in enumerate(arrays) if other is a) for a, _ in operands]
        out_views = [self.cut((out, 0), out.shape[-1] // self.groups)[1] for out in outs]

        def kernel(*refs):
            ins, results = refs[: len(arrays)], refs[len(refs) - len(outs) :]

            for group in range(self.groups):
                taken = [view(ins[place], group) for place, (_, view) in zip(places, operands)]
                given = [view(ref, group) for ref, view in zip(results, out_views)]
                extra = () if slots is None else (refs[len(arrays)],)
                body(self.reverse, self.spans, *taken, *given, *extra)

        whole = pl.BlockSpec(memory_space=pltpu.VMEM)
        index = [] if slots is None else [slots]
        return pl.pallas_call(
            kernel,
            in_specs=[whole] * len(arrays) + [pl.BlockSpec(memory_space=pltpu.SMEM)] * len(index),
            out_specs=[whole] * len(outs),
            out_shape=outs,
            compiler_params=pltpu.CompilerParams(vmem_limit_bytes=48 * 2**20),
            cost_estimate=pl.CostEstimate(
                flops=flops, bytes_accessed=2**22, transcendentals=0
            ),
        )(*arrays, *index)

    def states(self):
        self.before, total = self.call(
            states_kernel,
            [self.cut(self.values, self.cols), self.cut(self.keys, STATE), self.decay_cut()],
            [
                jax.ShapeDtypeStruct((max(self.spans - 1, 1), STATE, self.width), F32),
                jax.ShapeDtypeStruct((STATE, self.width), BF16),
            ],
            2 * self.tokens * STATE * self.width,
        )
        return total

    def inner(self):
        (self.near,) = self.call(
            inner_kernel,
            [
                self.cut(self.values, self.cols),
                self.cut(self.keys, STATE),
                self.cut(self.queries, STATE),
                self.decay_cut(),
            ],
            [jax.ShapeDtypeStruct((self.tokens, self.width), BF16)],
            8 * self.tokens * SPAN * self.width,
        )

    def finish(self, incoming, first, slots=None):
        shape = (self.tokens, self.width)
        if slots is not None:
            shape = (slots.shape[0], self.tokens // slots.shape[0], self.width)
        (result,) = self.call(
            finish_kernel,
            [
                self.cut((self.near, 0), self.cols),
                self.cut(self.queries, STATE),
                self.decay_cut(),
                self.cut((self.before, 0), self.cols),
                self.cut((incoming, first), self.cols),
            ],
            [jax.ShapeDtypeStruct(shape, BF16)],
            2 * self.tokens * STATE * self.width,
            slots,
        )
        return result


def prefix_kernel(directions, arrived_ref, factor_ref, out_ref):
    count, rows, width = out_ref.shape
    width //= len(directions)
    for place, reverse in enumerate(directions):
        cols = slice(place * width, (place + 1) * width)
        run = jnp.zeros((rows, width), F32)
        order = range(count)
        for index in order[::-1] if reverse else order:
            out_ref[index, :, cols] = run.astype(BF16)
            run = run * factor_ref[index, :, cols] + arrived_ref[index, :, cols].astype(F32)


def carried(totals, factors, directions, beside, sums=None):
    count = lax.axis_size("seq")
    total = jnp.concatenate(totals, axis=1)
    pieces = total.reshape(count, STATE // count, -1)
    if sums is not None:
        parts, rest = [], sums.reshape(-1)
        for _ in range(3):
            parts.append(lax.reduce_precision(rest, 8, 7))
            rest = rest - parts[-1]
        taken = sums.size
        row = jnp.concatenate(parts).astype(BF16)
        row = jnp.pad(row, (0, -row.size % LANES))
        row = jnp.broadcast_to(row, (*pieces.shape[:2], row.size))
        pieces = jnp.concatenate([pieces, row], axis=2)
    arrived = lax.all_to_all(pieces, "seq", split_axis=0, concat_axis=0, tiled=True)
    arrived, beside.near = lax.optimization_barrier((arrived, beside.near))
    if sums is not None:
        width = total.shape[1]
        rows = arrived[:, 0, width : width + 3 * taken].astype(F32).reshape(count, 3, taken)
        factors = jnp.exp(jnp.sum(rows, axis=1))[:, :, None]
        factors = jnp.broadcast_to(factors, (count, taken, HEAD_DIM)).reshape(count, 1, width)
    composed = pl.pallas_call(
        functools.partial(prefix_kernel, directions),
        out_shape=jax.ShapeDtypeStruct((*arrived.shape[:2], total.shape[1]), BF16),
    )(arrived, factors)
    back = lax.all_to_all(composed, "seq", split_axis=0, concat_axis=0, tiled=True)
    return back.reshape(total.shape), factors


def gather_kernel(counts, index_ref, *refs):
    sources, out_ref = refs[: len(counts)], refs[-1]

    @pl.loop(0, out_ref.shape[0])
    def _(unit):
        first = 0
        for source, width in zip(sources, counts):
            out_ref[unit, :, first : first + width] = source[index_ref[unit]]
            first += width


def gathered(arrays, index):
    widths = tuple(array.shape[2] for array in arrays)
    units, rows = arrays[0].shape[:2]
    whole = pl.BlockSpec(memory_space=pltpu.VMEM)
    return pl.pallas_call(
        functools.partial(gather_kernel, widths),
        in_specs=[pl.BlockSpec(memory_space=pltpu.SMEM)] + [whole] * len(arrays),
        out_specs=whole,
        out_shape=jax.ShapeDtypeStruct((units, rows, sum(widths)), arrays[0].dtype),
        compiler_params=pltpu.CompilerParams(vmem_limit_bytes=48 * 2**20),
    )(index, *arrays)


def inverse(order):
    count = order.shape[0]
    spots = jnp.arange(count, dtype=jnp.int32)
    return jnp.sum(jnp.where(order[None, :] == spots[:, None], spots[None, :], 0), axis=1)


def shards(
    ssm_input,
    input_map,
    output_map,
    decay_forward,
    decay_reverse,
    skip_gain,
    norm_gain,
    scan_order,
    raster_order,
    grad_normed,
):
    unit_count = scan_order.shape[0]
    tok_rows, width = ssm_input.shape
    unit_rows = tok_rows // unit_count
    maps = input_map.shape[1]
    groups = maps // STATE
    heads = decay_forward.shape[0]
    raster_dest = raster_order // unit_count
    scan_source = scan_order // unit_count
    send_scan = inverse(raster_dest)

    def units(array):
        return array.reshape(unit_count, unit_rows, -1)

    def swapped(outgoing):
        return lax.all_to_all(outgoing, "seq", split_axis=0, concat_axis=0, tiled=True)

    def sent(arrays, send_index):
        return swapped(gathered([units(array) for array in arrays], send_index))

    def placed(arrived, recv_index):
        return gathered([arrived], recv_index).reshape(tok_rows, -1)

    def padded(decay):
        wide = decay.astype(F32).reshape(groups, heads // groups, tok_rows)
        return jnp.pad(wide, ((0, 0), (0, PAD - heads // groups), (0, 0)))

    sums = jnp.stack([decay_forward, decay_reverse]).astype(F32).sum(axis=2)
    decay_f, decay_r = padded(decay_forward), padded(decay_reverse)

    keys_at, queries_at = width, width + maps

    arrived = sent([ssm_input, input_map, output_map], send_scan)
    ahead = Scan((ssm_input, 0), (input_map, 0), (output_map, 0), decay_f, width, False)
    ahead_total = ahead.states()
    ahead.inner()
    arrived, ahead_total, sums = lax.optimization_barrier((arrived, ahead_total, sums))
    joined = placed(arrived, scan_source)
    behind = Scan((joined, 0), (joined, keys_at), (joined, queries_at), decay_r, width, True)
    entering, factors = carried((ahead_total, behind.states()), None, (False, True), ahead, sums)
    behind.inner()
    y_reverse_sent = swapped(behind.finish(entering, width, scan_source))
    y_forward = ahead.finish(entering, 0)
    y_reverse = placed(y_reverse_sent, raster_dest)

    skip_cols = jnp.repeat(skip_gain, HEAD_DIM)
    combined = (
        y_forward.astype(F32) + y_reverse.astype(F32) + skip_cols * ssm_input.astype(F32)
    )
    scaled_grad = norm_gain * grad_normed.astype(F32)
    both = jnp.stack(
        [jnp.sum(combined * combined, axis=1), jnp.sum(combined * scaled_grad, axis=1)]
    )
    squares, inner_sum = lax.psum(both, "head")
    inv_rms = lax.rsqrt(squares / FEATURES + EPSILON)
    normed_output = (combined * inv_rms[:, None] * norm_gain).astype(BF16)
    grad_combined = (
        inv_rms[:, None] * scaled_grad - combined * (inv_rms**3 * inner_sum / FEATURES)[:, None]
    ).astype(BF16)

    arrived = sent([grad_combined], send_scan)
    ahead_grad = Scan((grad_combined, 0), (output_map, 0), (input_map, 0), decay_f, width, True)
    ahead_total = ahead_grad.states()
    ahead_grad.inner()
    arrived, ahead_total = lax.optimization_barrier((arrived, ahead_total))
    grad_scan = placed(arrived, scan_source)
    behind_grad = Scan((grad_scan, 0), (joined, queries_at), (joined, keys_at), decay_r, width, False)
    entering, _ = carried((ahead_total, behind_grad.states()), factors, (True, False), ahead_grad)
    behind_grad.inner()
    grad_reverse_sent = swapped(behind_grad.finish(entering, width, scan_source))
    grad_forward = ahead_grad.finish(entering, 0)
    grad_reverse = placed(grad_reverse_sent, raster_dest)

    grad_input = (
        grad_forward.astype(F32)
        + grad_reverse.astype(F32)
        + skip_cols * grad_combined.astype(F32)
    )
    return (normed_output, grad_input.astype(BF16))


def solution(mesh):
    return jax.shard_map(
        shards,
        mesh=mesh,
        in_specs=(
            P("seq", "head"),
            P("seq", "head"),
            P("seq", "head"),
            P("head", "seq"),
            P("head", "seq"),
            P("head"),
            P("head"),
            P("seq"),
            P("seq"),
            P("seq", "head"),
        ),
        out_specs=(P("seq", "head"), P("seq", "head")),
        check_vma=False,
    )
```

```python
import functools

import jax
import jax.numpy as jnp
from jax import lax
from jax.experimental import pallas as pl
from jax.experimental.pallas import tpu as pltpu
from jax.sharding import PartitionSpec as P

HEAD_DIM = 64
STATE = 128
SPAN = 256
FEATURES = 3072
PAD = 8
LANES = 128
EPSILON = 1e-05
F32 = jnp.float32
BF16 = jnp.bfloat16


def triangle(lower):
    rows = lax.broadcasted_iota(jnp.int32, (SPAN, SPAN), 0)
    cols = lax.broadcasted_iota(jnp.int32, (SPAN, SPAN), 1)
    return cols <= rows if lower else cols >= rows


def spread_pair(columns, pair):
    shape = (columns.shape[0], LANES)
    lane = lax.broadcasted_iota(jnp.int32, shape, 1)
    return jnp.where(
        lane < HEAD_DIM, columns[:, 2 * pair : 2 * pair + 1], columns[:, 2 * pair + 1 : 2 * pair + 2]
    )


def spread_heads(columns, pairs):
    return jnp.concatenate([spread_pair(columns, pair) for pair in range(pairs)], axis=1)


def running_columns(decay):
    ones = jnp.where(triangle(True), 1.0, 0.0).astype(BF16)
    return lax.dot_general(ones, decay, (((1,), (1,)), ((), ())), preferred_element_type=F32)


def running_rows(decay):
    ones = jnp.where(triangle(False), 1.0, 0.0).astype(BF16)
    return jnp.dot(decay, ones, preferred_element_type=F32)


def states_kernel(reverse, spans, v_ref, k_ref, decay_ref, before_ref, total_ref):
    pairs = v_ref.shape[1] // LANES
    order = range(spans)
    run = None
    for span in order[::-1] if reverse else order:
        rows = slice(span * SPAN, (span + 1) * SPAN)
        cum = running_columns(decay_ref[0, :, rows].astype(BF16))
        end = cum[SPAN - 1 : SPAN]
        weight = jnp.exp(cum) if reverse else jnp.exp(end - cum)
        scaled = (v_ref[rows, :].astype(F32) * spread_heads(weight, pairs)).astype(BF16)
        state = lax.dot_general(
            k_ref[rows, :], scaled, (((0,), (0,)), ((), ())), preferred_element_type=F32
        )
        if run is None:
            run = state
        else:
            before_ref[span if reverse else span - 1] = run
            run = run * spread_heads(jnp.exp(end), pairs) + state
    total_ref[...] = run.astype(BF16)


def inner_kernel(reverse, spans, v_ref, k_ref, q_ref, decay_ref, out_ref):
    pairs = v_ref.shape[1] // LANES
    allowed = triangle(not reverse)
    lane = lax.broadcasted_iota(jnp.int32, (SPAN, LANES), 1)
    for span in range(spans):
        rows = slice(span * SPAN, (span + 1) * SPAN)
        decay = decay_ref[0, :, rows].astype(BF16)
        cum_col = running_columns(decay)
        cum_row = running_rows(decay)
        scores = lax.dot_general(
            q_ref[rows, :], k_ref[rows, :], (((1,), (1,)), ((), ())), preferred_element_type=F32
        )
        scores = jnp.where(allowed, scores, 0.0)
        for pair in range(pairs):
            values = v_ref[rows, pair * LANES : (pair + 1) * LANES]
            parts = []
            for head in (2 * pair, 2 * pair + 1):
                col, row = cum_col[:, head : head + 1], cum_row[head : head + 1, :]
                gap = row - col if reverse else col - row
                weights = (scores * jnp.exp(jnp.minimum(gap, 0.0))).astype(BF16)
                parts.append(jnp.dot(weights, values, preferred_element_type=F32))
            out_ref[rows, pair * LANES : (pair + 1) * LANES] = jnp.where(
                lane < HEAD_DIM, parts[0], parts[1]
            ).astype(BF16)


def finish_kernel(reverse, spans, inner_ref, q_ref, decay_ref, before_ref, incoming_ref, out_ref, slot_ref=None):
    pairs = inner_ref.shape[1] // LANES
    order = range(spans)
    incoming = incoming_ref[...].astype(F32)
    passed = None
    for span in order[::-1] if reverse else order:
        rows = slice(span * SPAN, (span + 1) * SPAN)
        cum = running_columns(decay_ref[0, :, rows].astype(BF16))
        end = cum[SPAN - 1 : SPAN]
        weight = jnp.exp(end - cum) if reverse else jnp.exp(cum)
        if passed is None:
            entering = incoming
            passed = end
        else:
            entering = before_ref[span if reverse else span - 1] + incoming * spread_heads(jnp.exp(passed), pairs)
            passed = passed + end
        outer = jnp.dot(q_ref[rows, :], entering.astype(BF16), preferred_element_type=F32)
        total = inner_ref[rows, :].astype(F32) + outer * spread_heads(weight, pairs)
        if slot_ref is None:
            out_ref[rows, :] = total.astype(BF16)
            continue
        unit_rows = out_ref.shape[1]
        per_span = SPAN // unit_rows
        for unit in range(per_span):
            piece = total[unit * unit_rows : (unit + 1) * unit_rows]
            out_ref[slot_ref[span * per_span + unit]] = piece.astype(BF16)


class Scan:
    def __init__(self, values, keys, queries, decay, width, reverse):
        self.decay, self.reverse, self.width = decay, reverse, width
        self.groups = decay.shape[0]
        self.tokens = decay.shape[2]
        self.spans = self.tokens // SPAN
        self.cols = width // self.groups
        self.values, self.keys, self.queries = values, keys, queries

    def cut(self, operand, size):
        array, first = operand
        lead = (slice(None),) * (array.ndim - 1)

        def view(ref, group):
            at = first + group * size
            at = at if isinstance(group, int) else pl.multiple_of(at, LANES)
            return ref.at[(*lead, pl.ds(at, size))]

        return array, view

    def decay_cut(self):
        return self.decay, lambda ref, group: ref.at[pl.ds(group, 1)]

    def call(self, body, operands, outs, flops, slots=None):
        arrays = []
        for array, _ in operands:
            if not any(array is other for other in arrays):
                arrays.append(array)
        places = [next(i for i, other in enumerate(arrays) if other is a) for a, _ in operands]
        out_views = [self.cut((out, 0), out.shape[-1] // self.groups)[1] for out in outs]

        def kernel(*refs):
            ins, results = refs[: len(arrays)], refs[len(refs) - len(outs) :]

            def step(group):
                taken = [view(ins[place], group) for place, (_, view) in zip(places, operands)]
                given = [view(ref, group) for ref, view in zip(results, out_views)]
                extra = () if slots is None else (refs[len(arrays)],)
                body(self.reverse, self.spans, *taken, *given, *extra)

            if body is inner_kernel:
                pl.loop(0, self.groups)(step)
            else:
                for group in range(self.groups):
                    step(group)

        whole = pl.BlockSpec(memory_space=pltpu.VMEM)
        index = [] if slots is None else [slots]
        return pl.pallas_call(
            kernel,
            in_specs=[whole] * len(arrays) + [pl.BlockSpec(memory_space=pltpu.SMEM)] * len(index),
            out_specs=[whole] * len(outs),
            out_shape=outs,
            compiler_params=pltpu.CompilerParams(vmem_limit_bytes=48 * 2**20),
            cost_estimate=pl.CostEstimate(
                flops=flops, bytes_accessed=2**22, transcendentals=0
            ),
        )(*arrays, *index)

    def states(self):
        self.before, total = self.call(
            states_kernel,
            [self.cut(self.values, self.cols), self.cut(self.keys, STATE), self.decay_cut()],
            [
                jax.ShapeDtypeStruct((max(self.spans - 1, 1), STATE, self.width), F32),
                jax.ShapeDtypeStruct((STATE, self.width), BF16),
            ],
            2 * self.tokens * STATE * self.width,
        )
        return total

    def inner(self):
        (self.near,) = self.call(
            inner_kernel,
            [
                self.cut(self.values, self.cols),
                self.cut(self.keys, STATE),
                self.cut(self.queries, STATE),
                self.decay_cut(),
            ],
            [jax.ShapeDtypeStruct((self.tokens, self.width), BF16)],
            8 * self.tokens * SPAN * self.width,
        )

    def finish(self, incoming, first, slots=None):
        shape = (self.tokens, self.width)
        if slots is not None:
            shape = (slots.shape[0], self.tokens // slots.shape[0], self.width)
        (result,) = self.call(
            finish_kernel,
            [
                self.cut((self.near, 0), self.cols),
                self.cut(self.queries, STATE),
                self.decay_cut(),
                self.cut((self.before, 0), self.cols),
                self.cut((incoming, first), self.cols),
            ],
            [jax.ShapeDtypeStruct(shape, BF16)],
            2 * self.tokens * STATE * self.width,
            slots,
        )
        return result


def prefix_kernel(directions, arrived_ref, factor_ref, out_ref):
    count, rows, width = out_ref.shape
    width //= len(directions)
    for place, reverse in enumerate(directions):
        cols = slice(place * width, (place + 1) * width)
        run = jnp.zeros((rows, width), F32)
        order = range(count)
        for index in order[::-1] if reverse else order:
            out_ref[index, :, cols] = run.astype(BF16)
            run = run * factor_ref[index, :, cols] + arrived_ref[index, :, cols].astype(F32)


def carried(totals, factors, directions, beside, sums=None):
    count = lax.axis_size("seq")
    total = jnp.concatenate(totals, axis=1)
    pieces = total.reshape(count, STATE // count, -1)
    if sums is not None:
        parts, rest = [], sums.reshape(-1)
        for _ in range(3):
            parts.append(lax.reduce_precision(rest, 8, 7))
            rest = rest - parts[-1]
        taken = sums.size
        row = jnp.concatenate(parts).astype(BF16)
        row = jnp.pad(row, (0, -row.size % LANES))
        row = jnp.broadcast_to(row, (*pieces.shape[:2], row.size))
        pieces = jnp.concatenate([pieces, row], axis=2)
    arrived = lax.all_to_all(pieces, "seq", split_axis=0, concat_axis=0, tiled=True)
    arrived, beside.near = lax.optimization_barrier((arrived, beside.near))
    if sums is not None:
        width = total.shape[1]
        rows = arrived[:, 0, width : width + 3 * taken].astype(F32).reshape(count, 3, taken)
        factors = jnp.exp(jnp.sum(rows, axis=1))[:, :, None]
        factors = jnp.broadcast_to(factors, (count, taken, HEAD_DIM)).reshape(count, 1, width)
    composed = pl.pallas_call(
        functools.partial(prefix_kernel, directions),
        out_shape=jax.ShapeDtypeStruct((*arrived.shape[:2], total.shape[1]), BF16),
    )(arrived, factors)
    back = lax.all_to_all(composed, "seq", split_axis=0, concat_axis=0, tiled=True)
    return back.reshape(total.shape), factors


def gather_kernel(counts, index_ref, *refs):
    sources, out_ref = refs[: len(counts)], refs[-1]

    @pl.loop(0, out_ref.shape[0])
    def _(unit):
        first = 0
        for source, width in zip(sources, counts):
            out_ref[unit, :, first : first + width] = source[index_ref[unit]]
            first += width


def gathered(arrays, index):
    widths = tuple(array.shape[2] for array in arrays)
    units, rows = arrays[0].shape[:2]
    whole = pl.BlockSpec(memory_space=pltpu.VMEM)
    return pl.pallas_call(
        functools.partial(gather_kernel, widths),
        in_specs=[pl.BlockSpec(memory_space=pltpu.SMEM)] + [whole] * len(arrays),
        out_specs=whole,
        out_shape=jax.ShapeDtypeStruct((units, rows, sum(widths)), arrays[0].dtype),
        compiler_params=pltpu.CompilerParams(vmem_limit_bytes=48 * 2**20),
    )(index, *arrays)


def inverse(order):
    count = order.shape[0]
    spots = jnp.arange(count, dtype=jnp.int32)
    return jnp.sum(jnp.where(order[None, :] == spots[:, None], spots[None, :], 0), axis=1)


def shards(
    ssm_input,
    input_map,
    output_map,
    decay_forward,
    decay_reverse,
    skip_gain,
    norm_gain,
    scan_order,
    raster_order,
    grad_normed,
):
    unit_count = scan_order.shape[0]
    tok_rows, width = ssm_input.shape
    unit_rows = tok_rows // unit_count
    maps = input_map.shape[1]
    groups = maps // STATE
    heads = decay_forward.shape[0]
    raster_dest = raster_order // unit_count
    scan_source = scan_order // unit_count
    send_scan = inverse(raster_dest)
    send_raster = inverse(scan_source)

    def units(array):
        return array.reshape(unit_count, unit_rows, -1)

    def swapped(outgoing):
        return lax.all_to_all(outgoing, "seq", split_axis=0, concat_axis=0, tiled=True)

    def sent(arrays, send_index):
        return swapped(gathered([units(array) for array in arrays], send_index))

    def placed(arrived, recv_index):
        return gathered([arrived], recv_index).reshape(tok_rows, -1)

    def padded(decay):
        wide = decay.astype(F32).reshape(groups, heads // groups, tok_rows)
        return jnp.pad(wide, ((0, 0), (0, PAD - heads // groups), (0, 0)))

    sums = jnp.stack([decay_forward, decay_reverse]).astype(F32).sum(axis=2)
    decay_f, decay_r = padded(decay_forward), padded(decay_reverse)

    keys_at, queries_at = width, width + maps

    arrived = sent([ssm_input, input_map, output_map], send_scan)
    ahead = Scan((ssm_input, 0), (input_map, 0), (output_map, 0), decay_f, width, False)
    ahead_total = ahead.states()
    ahead.inner()
    arrived, ahead_total, sums = lax.optimization_barrier((arrived, ahead_total, sums))
    joined = placed(arrived, scan_source)
    behind = Scan((joined, 0), (joined, keys_at), (joined, queries_at), decay_r, width, True)
    entering, factors = carried((ahead_total, behind.states()), None, (False, True), ahead, sums)
    behind.inner()
    y_reverse_sent = sent([behind.finish(entering, width)], send_raster)
    y_forward = ahead.finish(entering, 0)
    y_reverse = placed(y_reverse_sent, raster_dest)

    skip_cols = jnp.repeat(skip_gain, HEAD_DIM)
    combined = (
        y_forward.astype(F32) + y_reverse.astype(F32) + skip_cols * ssm_input.astype(F32)
    )
    scaled_grad = norm_gain * grad_normed.astype(F32)
    both = jnp.stack(
        [jnp.sum(combined * combined, axis=1), jnp.sum(combined * scaled_grad, axis=1)]
    )
    squares, inner_sum = lax.psum(both, "head")
    inv_rms = lax.rsqrt(squares / FEATURES + EPSILON)
    normed_output = (combined * inv_rms[:, None] * norm_gain).astype(BF16)
    grad_combined = (
        inv_rms[:, None] * scaled_grad - combined * (inv_rms**3 * inner_sum / FEATURES)[:, None]
    ).astype(BF16)

    arrived = sent([grad_combined], send_scan)
    ahead_grad = Scan((grad_combined, 0), (output_map, 0), (input_map, 0), decay_f, width, True)
    ahead_total = ahead_grad.states()
    ahead_grad.inner()
    arrived, ahead_total = lax.optimization_barrier((arrived, ahead_total))
    grad_scan = placed(arrived, scan_source)
    behind_grad = Scan((grad_scan, 0), (joined, queries_at), (joined, keys_at), decay_r, width, False)
    entering, _ = carried((ahead_total, behind_grad.states()), factors, (True, False), ahead_grad)
    behind_grad.inner()
    grad_reverse_sent = sent([behind_grad.finish(entering, width)], send_raster)
    grad_forward = ahead_grad.finish(entering, 0)
    grad_reverse = placed(grad_reverse_sent, raster_dest)

    grad_input = (
        grad_forward.astype(F32)
        + grad_reverse.astype(F32)
        + skip_cols * grad_combined.astype(F32)
    )
    return (normed_output, grad_input.astype(BF16))


def solution(mesh):
    return jax.shard_map(
        shards,
        mesh=mesh,
        in_specs=(
            P("seq", "head"),
            P("seq", "head"),
            P("seq", "head"),
            P("head", "seq"),
            P("head", "seq"),
            P("head"),
            P("head"),
            P("seq"),
            P("seq"),
            P("seq", "head"),
        ),
        out_specs=(P("seq", "head"), P("seq", "head")),
        check_vma=False,
    )
```
